512 devices in a mesh: section: 8 (over x, y_lo), dp: 64 (over y_hi, z, core).
Axes of the slice: x: 4, y: 8 (y_hi: 4, y_lo: 2; y = y_hi * 2 + y_lo), z: 8, core: 2. Of those that a mesh axis runs over, the one named last changes fastest.
Arguments:
- saved: bfloat16 [8, 2, 8192, 4096], P('section', None, 'dp'), may hold values from -6 to 6
- top_grad: bfloat16 [2, 8192, 4096], P(None, 'dp'), may hold values from -0.4375 to 0.4375
- gains: float32 [8, 2, 4096], P('section'), may hold values from 0.1 to 1.9
- adapter_in: bfloat16 [8, 2, 4096, 32], P('section'), may hold values from -0.09375 to 0.09375
- adapter_out: bfloat16 [8, 2, 32, 4096], P('section'), may hold values from -1 to 1
Outputs:
- grad_in: float32 [8, 4096, 32], P('section', 'dp')
- grad_out: float32 [8, 32, 4096], P('section', None, 'dp')
The draws below stay inside these ranges and needn't reach their ends.
All inputs are finite; a program needn't handle non-finite values.
Results may differ from the reference program's by a relative error of at most 0.014.
Values may be sent and summed in bfloat16 or wider, within the bound.
A program may use at most 64 MiB of HBM per device.

```python
import jax
import jax.numpy as jnp
from jax import lax

D = 4096
RANK = 32
SECTIONS = 8
TOKENS = 8192
N_SECTION = 8


def raised(array, own_key, source, target, blocks, factor):
    def block_of(position):
        return (jnp.arange(array.shape[position]) // (array.shape[position] // blocks)).reshape((-1,) + (1,) * (array.ndim - 1 - position))

    first = jax.random.permutation(own_key, blocks)[block_of(target)]
    second = (block_of(target) + blocks // 2) % blocks
    return jnp.where((block_of(source) == first) | (block_of(source) == second), factor * array, array)


def shard_levels(stream_key, extent, split, low, largest):
    level = 1.0
    for position, shards_of in split:
        heights = jax.random.uniform(jax.random.fold_in(jax.random.fold_in(stream_key, 6), position), (shards_of,), jnp.float32, low / len(split), largest / len(split))
        level = level * jnp.repeat(jnp.exp(heights), extent[position] // shards_of).reshape((-1,) + (1,) * (len(extent) - 1 - position))
    return level


def bell_draw(stream_key, extent, width, bound, pieces=(), kind=jnp.bfloat16):
    loudness = shard_levels(stream_key, extent, pieces, -0.22, 0.18) if pieces else 1.0
    entries = jax.random.normal(stream_key, extent, jnp.float32) * width * loudness
    return jnp.minimum(jnp.maximum(entries, -bound), bound).astype(kind)


def heavy_noise(own_key, dims, spread, reach, split, heavy, dtype=jnp.bfloat16):
    drawn = spread * jax.random.normal(own_key, dims, jnp.float32)
    if split:
        drawn = drawn * shard_levels(own_key, dims, split, -0.22, 0.18)
    return jnp.clip(raised(drawn, jax.random.fold_in(own_key, 3), *heavy), -reach, reach).astype(dtype)


def setup_inputs(seed: int = 0) -> dict:
    arg_keys = jax.random.split(jax.random.key(seed), 6)
    return {
        "saved": bell_draw(arg_keys[0], (SECTIONS, 2, TOKENS, D), 1.0, 6.0, ((0, 8), (2, 64))),
        "top_grad": heavy_noise(arg_keys[1], (2, TOKENS, D), (TOKENS ** -0.5), 0.4375, ((1, 64),), (1, 2, 64, 4.0)),
        "gains": jnp.clip(1.0 + 0.18 * jax.random.normal(arg_keys[2], (SECTIONS, 2, D), jnp.float32), 0.1, 1.9),
        "adapter_in": bell_draw(arg_keys[3], (SECTIONS, 2, D, RANK), D ** -0.5, 0.09375, ((0, 8),)),
        "adapter_out": bell_draw(arg_keys[4], (SECTIONS, 2, RANK, D), RANK ** -0.5, 1.0, ((0, 8),)),
    }


EPS = 1e-05

def section_back(x, upstream, gain, weight_in, weight_out):
    xf = x.astype(jnp.float32)
    scale = lax.rsqrt(lax.optimization_barrier(jnp.mean(xf * xf, axis=-1, keepdims=True)) + EPS)
    normed = xf * scale
    hidden = (normed * gain).astype(jnp.bfloat16)
    pre = jnp.dot(hidden, weight_in, preferred_element_type=jnp.float32)
    sig = jax.nn.sigmoid(pre)
    active = (pre * sig).astype(jnp.bfloat16)
    delta_act = jnp.dot(upstream, weight_out.T, preferred_element_type=jnp.float32)
    delta_pre = (delta_act * sig * (1.0 + pre * (1.0 - sig))).astype(jnp.bfloat16)
    delta_hidden = jnp.dot(delta_pre, weight_in.T, preferred_element_type=jnp.float32)
    delta_norm = delta_hidden * gain
    inner = lax.optimization_barrier(jnp.mean(delta_norm * normed, axis=-1, keepdims=True))
    result = (upstream.astype(jnp.float32) + scale * (delta_norm - normed * inner)).astype(jnp.bfloat16)
    term_in = jnp.dot(hidden.T, delta_pre, preferred_element_type=jnp.float32)
    term_out = jnp.dot(active.T, upstream, preferred_element_type=jnp.float32)
    return (result, term_in, term_out)

def reference(saved, top_grad, gains, adapter_in, adapter_out):
    sections = N_SECTION
    sums_in = [jnp.zeros((D, RANK), jnp.float32) for j in range(sections)]
    sums_out = [jnp.zeros((RANK, D), jnp.float32) for j in range(sections)]
    for replica in range(2):
        upstream = top_grad[replica]
        for j in reversed(range(sections)):
            where = j if replica == 0 else sections - 1 - j
            upstream, term_in, term_out = section_back(saved[where, replica], upstream, gains[where, replica], adapter_in[where, replica], adapter_out[where, replica])
            sums_in[j] = sums_in[j] + term_in
            sums_out[j] = sums_out[j] + term_out
    return (jnp.stack(sums_in), jnp.stack(sums_out))
```

```python
from functools import partial

import jax
import jax.numpy as jnp
from jax import lax
from jax.experimental import pallas as pl
from jax.experimental.pallas import tpu as pltpu
from jax.sharding import PartitionSpec as P

EPS = 1e-05
CORES = 2
RINGS = {64: (4, 8), 8: (2, 2), 4: (1, 2)}
BF16 = jnp.bfloat16
F32 = jnp.float32


def over_last(a, b):
    return lax.dot_general(a, b, (((1,), (1,)), ((), ())), preferred_element_type=F32)


def dot(a, b):
    return jnp.dot(a, b, preferred_element_type=F32)


def kernel(
    dims, saved, top, gains, win, wout, out_in, out_out,
    xv, tv, hv, gv, iv, ov, wall, scale_v, msg, coup, got, cgot, ans, back,
    es, pe, ss, sr, fr, zs, zr, zt, yr, fin,
    load_sem, w_send, w_recv, o_send, o_recv, m_send, m_recv, k_send, k_recv,
    a_send, a_recv, c_send, c_recv, s_send, s_recv, f_send, f_recv,
    z_send, z_recv, y_send, y_recv, e_send, e_recv,
):
    S, NY, NZ, T, D, R = dims
    NL = S * R
    H = R // 2
    Q = T // S
    CH = D // NY
    me = lax.axis_index("section")
    dp = lax.axis_index("dp")
    core = lax.rem(dp, CORES)
    z = lax.rem(dp // CORES, NZ)
    yh = dp // (CORES * NZ)
    mate = dp + 1 - 2 * core
    mirror = S - 1 - me

    def on_section(j):
        return {"section": j, "dp": dp}

    def on_dp(k):
        return {"section": me, "dp": k}

    def z_peer(k):
        return yh * (NZ * CORES) + k * CORES + core

    def y_peer(k):
        return k * (NZ * CORES) + z * CORES + core

    def peer(i):
        return lax.rem(me + i, S)

    def remote(src, dst, send, recv, device):
        return pltpu.make_async_remote_copy(
            src_ref=src, dst_ref=dst, send_sem=send, recv_sem=recv,
            device_id=device, device_id_type=pl.DeviceIdType.MESH,
        )

    loads = []
    for r in range(2):
        rows = pl.ds(r * T, T)
        loads.append(pltpu.make_async_copy(saved.at[0, r], xv.at[rows], load_sem.at[r]))
    loads.append(pltpu.make_async_copy(gains.at[0], gv, load_sem.at[2]))
    loads.append(pltpu.make_async_copy(win.at[0], iv, load_sem.at[3]))
    loads.append(pltpu.make_async_copy(wout.at[0], ov, load_sem.at[4]))
    for r in range(2):
        rows = pl.ds(r * T, T)
        loads.append(pltpu.make_async_copy(top.at[r], tv.at[rows], load_sem.at[5 + r]))
    for copy in loads:
        copy.start()

    barrier = pltpu.get_barrier_semaphore()
    greeted = [on_section(peer(i)) for i in range(1, S)] + [on_dp(mate)]
    greeted += [on_dp(z_peer(lax.rem(z + i, NZ))) for i in range(1, NZ)]
    greeted += [on_dp(y_peer(lax.rem(yh + i, NY))) for i in range(1, NY)]
    for device in greeted:
        pl.semaphore_signal(barrier, inc=1, device_id=device, device_id_type=pl.DeviceIdType.MESH)
    pl.semaphore_wait(barrier, len(greeted))

    half = pl.ds(pl.multiple_of(core * H, H), H)
    other_half = pl.ds(pl.multiple_of((1 - core) * H, H), H)
    w_copies = []
    for i in range(1, S):
        j = peer(i)
        replica = jnp.where(j > me, 0, 1)
        copy = remote(
            wout.at[0, replica, half], wall.at[me, half], w_send.at[i], w_recv.at[me], on_section(j)
        )
        copy.start()
        w_copies.append(copy)

    for n in range(5):
        loads[n].wait()
    wall[me] = ov[0]

    W = 512

    def squares(i, acc):
        xf = xv[:, pl.ds(pl.multiple_of(i * 128, 128), 128)].astype(F32)
        return acc + xf * xf

    total = lax.fori_loop(0, D // 128, squares, jnp.zeros((2 * T, 128), F32), unroll=2)
    scale = lax.rsqrt(jnp.sum(total, axis=-1, keepdims=True) * (1.0 / D) + EPS)
    scale_v[...] = jnp.broadcast_to(scale, (2 * T, 128))

    def normed(i, carry):
        cols = pl.ds(pl.multiple_of(i * 128, 128), 128)
        for r in range(2):
            rows = slice(r * T, (r + 1) * T)
            nf = xv[rows, cols].astype(F32) * scale_v[rows, :]
            hv[rows, cols] = (nf * gv[r : r + 1, cols]).astype(BF16)
        return carry

    lax.fori_loop(0, D // 128, normed, 0)
    for n in range(5, 7):
        loads[n].wait()
    for r in range(2):
        rows = slice(r * T, (r + 1) * T)
        msg[:, NL + r * R : NL + (r + 1) * R] = over_last(hv[rows, :], iv[r])
        msg[:, NL + (2 + r) * R : NL + (3 + r) * R] = over_last(tv[rows, :], ov[r])
    gained = jnp.concatenate(
        [(iv[r].astype(F32) * gv[r : r + 1, :]).astype(BF16) for r in range(2)], axis=0
    )

    def fills(k, j):
        return (j != k) & ((j < k) | (j < S - 1 - k))

    for k in range(S):
        @pl.when(jnp.logical_not(fills(k, me)))
        def _():
            sr[k] = jnp.zeros((H, D), BF16)

    o_copies = []
    for i in range(1, S):
        j = peer(S - i)
        remote(wall.at[j, half], wall.at[j, half], w_send.at[i], w_recv.at[j], on_section(j)).wait_recv()
        copy = remote(wall.at[j, half], wall.at[j, half], o_send.at[i], o_recv.at[j], on_dp(mate))
        copy.start()
        o_copies.append(copy)
    for i in range(1, S):
        j = peer(S - i)
        remote(
            wall.at[j, other_half], wall.at[j, other_half], o_send.at[i], o_recv.at[j], on_dp(mate)
        ).wait_recv()

    every = wall[...].reshape(NL, D)
    through = over_last(gained, every)
    block = lax.broadcasted_iota(jnp.int32, (R, NL), 1) // R
    coup[...] = jnp.where(block < me, through[:R], through[R:]).astype(BF16)
    k_copies = []
    for i in range(1, S):
        j = peer(i)
        copy = remote(coup, cgot.at[me], k_send.at[i], k_recv.at[me], on_section(j))
        copy.start()
        k_copies.append(copy)
    cgot[me] = coup[...]

    across = over_last(xv[...], every)
    lane = lax.broadcasted_iota(jnp.int32, (T, NL), 1)
    block = lane // R
    sc0 = scale_v[:T, 0:1]
    sc1 = scale_v[T:, 0:1]
    own = jnp.where(lax.rem(lane, R) < H, sc0, sc1)
    msg[:, :NL] = jnp.where(
        block < me, across[:T] * (sc0 * sc0), jnp.where(block > me, across[T:] * (sc1 * sc1), own)
    )
    m_copies = []
    for i in range(1, S):
        j = peer(i)
        rows = pl.ds(pl.multiple_of(j * Q, Q), Q)
        copy = remote(msg.at[rows], got.at[me], m_send.at[i], m_recv.at[me], on_section(j))
        copy.start()
        m_copies.append(copy)
    got[me] = msg[pl.ds(pl.multiple_of(me * Q, Q), Q), :]
    for i in range(1, S):
        j = peer(S - i)
        remote(coup, cgot.at[j], k_send.at[i], k_recv.at[j], on_section(j)).wait_recv()
        remote(msg.at[pl.ds(0, Q)], got.at[j], m_send.at[i], m_recv.at[j], on_section(j)).wait_recv()

    pre = got[:, :, NL : NL + 2 * R]
    sig = jax.nn.sigmoid(pre)
    active = pre * sig
    slope = sig * (1.0 + pre * (1.0 - sig))
    acc = [jnp.zeros((Q, NL), F32), jnp.zeros((Q, NL), F32)]
    for turn in range(S):
        for r in range(2):
            k = S - 1 - turn if r == 0 else turn
            lanes = slice(r * R, (r + 1) * R)
            up = got[k, :, NL + (2 + r) * R : NL + (3 + r) * R]
            if turn > 0:
                up = up + acc[r][:, k * R : (k + 1) * R]
            delta = (up * slope[k, :, lanes]).astype(BF16)
            inner = jnp.sum(delta.astype(F32) * pre[k, :, lanes], axis=-1, keepdims=True) * (1.0 / D)
            ans[k, :, 2 * NL + r * R : 2 * NL + (r + 1) * R] = delta
            if turn < S - 1:
                sc = got[k, :, k * R + r * H : k * R + r * H + 1]
                acc[r] = acc[r] + sc * dot(delta, cgot[k]) - inner * got[k, :, :NL]
    for k in range(S):
        ans[0, :, k * R : (k + 1) * R] = active[k, :, :R].astype(BF16)
        ans[0, :, NL + k * R : NL + (k + 1) * R] = active[S - 1 - k, :, R:].astype(BF16)
    both = ans[0, :, : 2 * NL]
    for k in range(1, S):
        ans[k, :, : 2 * NL] = both
    a_copies = []
    mine = pl.ds(pl.multiple_of(me * Q, Q), Q)
    for i in range(1, S):
        j = peer(i)
        copy = remote(ans.at[j], back.at[me], a_send.at[i], a_recv.at[me], on_section(j))
        copy.start()
        a_copies.append(copy)
    back[me] = ans[me]
    for i in range(1, S):
        j = peer(S - i)
        remote(ans.at[j], back.at[j], a_send.at[i], a_recv.at[j], on_section(j)).wait_recv()

    answer = back[...].reshape(T, 2 * NL + 2 * R)
    block = lax.broadcasted_iota(jnp.int32, (T, NL), 1) // R
    first = answer[:, :NL].astype(F32)
    second = answer[:, NL : 2 * NL].astype(F32)
    low = jnp.concatenate(
        [jnp.where(block < me, first, 0.0), jnp.where(block < mirror, second, 0.0)], axis=0
    ).T.astype(BF16)
    same = jnp.concatenate(
        [jnp.where(block == me, first, 0.0), jnp.where(block == me, second, 0.0)], axis=0
    ).T.astype(BF16)
    deltas = [answer[:, 2 * NL + r * R : 2 * NL + (r + 1) * R] for r in range(2)]
    turned = [delta.astype(F32).T.astype(BF16) for delta in deltas]
    pulls = []
    for r in range(2):
        rows = slice(r * T, (r + 1) * T)
        pre = msg[:, NL + r * R : NL + (r + 1) * R]
        inner = jnp.sum(deltas[r].astype(F32) * pre, axis=-1, keepdims=True) * (1.0 / D)
        pulls.append(inner * scale_v[rows, 0:1])

    N = S * H
    W = min(512, CH)
    c_copies = []
    for q in range(NY):
        def part(i, carry):
            cols = pl.ds(pl.multiple_of(q * CH + i * W, W), W)
            flow = []
            for r in range(2):
                rows = slice(r * T, (r + 1) * T)
                dn = dot(deltas[r], iv[r, :, cols]) * gv[r : r + 1, cols]
                change = scale_v[rows, 0:1] * (dn - pulls[r] * xv[rows, cols].astype(F32))
                flow.append(change.astype(BF16))
                term = dot(turned[r], hv[rows, cols]).astype(BF16)
                for h in range(2):
                    es[h, N + r * H : N + (r + 1) * H, cols] = term[h * H : (h + 1) * H]
            terms = (dot(low, jnp.concatenate(flow, axis=0)) + dot(same, tv[:, cols])).astype(BF16)
            for j in range(S):
                for h in range(2):
                    es[h, j * H : (j + 1) * H, cols] = terms[j * R + h * H : j * R + (h + 1) * H]
            return carry

        lax.fori_loop(0, CH // W, part, 0)
        cols = pl.ds(q * CH, CH)
        copy = remote(es.at[1 - core, :, cols], pe.at[:, cols], c_send.at[q], c_recv.at[q], on_dp(mate))
        copy.start()
        c_copies.append(copy)

    def section_copy(i, q):
        j = peer(i)
        cols = pl.ds(q * CH, CH)
        rows = pl.ds(pl.multiple_of(j * H, H), H)
        return j, remote(
            ss.at[rows, cols], sr.at[me, :, cols], s_send.at[i, q], s_recv.at[me, q], on_section(j)
        )

    def mirror_copy(q):
        cols = pl.ds(q * CH, CH)
        return remote(
            ss.at[pl.ds(N + H, H), cols], fr.at[:, cols], f_send.at[q], f_recv.at[q], on_section(mirror)
        )

    for q in range(NY):
        cols = pl.ds(q * CH, CH)
        c_copies[q].wait_recv()
        ss[:, cols] = (es[core, :, cols].astype(F32) + pe[:, cols].astype(F32)).astype(BF16)
        for i in range(1, S):
            j, copy = section_copy(i, q)

            @pl.when(fills(me, j))
            def _():
                copy.start()
        mirror_copy(q).start()

    def z_copy(i, q):
        k = lax.rem(z + i, NZ)
        source = pl.ds(pl.multiple_of(q * CH + k * 128, 128), 128)
        return remote(
            zs.at[:, source], zr.at[z, :, pl.ds(q * 128, 128)],
            z_send.at[i, q], z_recv.at[z, q], on_dp(z_peer(k)),
        )

    for q in range(NY):
        cols = pl.ds(q * CH, CH)
        for k in range(S):
            @pl.when(fills(k, me))
            def _():
                remote(
                    ss.at[pl.ds(0, H), cols], sr.at[k, :, cols],
                    s_send.at[0, q], s_recv.at[k, q], on_section(peer(1)),
                ).wait_recv()
        mirror_copy(q).wait_recv()
        own_rows = pl.ds(pl.multiple_of(me * H, H), H)
        whole = ss[own_rows, cols].astype(F32)
        for k in range(S):
            whole = whole + sr[k, :, cols].astype(F32)
        zs[0:H, cols] = whole.astype(BF16)
        zs[H:R, cols] = (ss[N : N + H, cols].astype(F32) + fr[:, cols].astype(F32)).astype(BF16)
        for i in range(1, NZ):
            z_copy(i, q).start()
        zr[z, :, q * 128 : (q + 1) * 128] = zs[:, pl.ds(pl.multiple_of(q * CH + z * 128, 128), 128)]

    def y_copy(q):
        return remote(zt.at[q], yr.at[yh], y_send.at[q], y_recv.at[yh], on_dp(y_peer(q)))

    for q in range(NY):
        for i in range(1, NZ):
            k = lax.rem(z + i, NZ)
            remote(
                zs.at[:, pl.ds(0, 128)], zr.at[k, :, pl.ds(q * 128, 128)],
                z_send.at[i, q], z_recv.at[k, q], on_dp(z_peer(k)),
            ).wait_recv()
        whole = zr[0, :, q * 128 : (q + 1) * 128].astype(F32)
        for k in range(1, NZ):
            whole = whole + zr[k, :, q * 128 : (q + 1) * 128].astype(F32)
        zt[q] = whole

        @pl.when(yh != q)
        def _():
            y_copy(q).start()

        @pl.when(yh == q)
        def _():
            yr[q] = zt[q]

    for k in range(NY):
        @pl.when(yh != k)
        def _():
            remote(zt.at[k], yr.at[k], y_send.at[k], y_recv.at[k], on_dp(y_peer(k))).wait_recv()

    whole = yr[0]
    for k in range(1, NY):
        whole = whole + yr[k]
    fin[core] = whole
    last = remote(fin.at[core], fin.at[core], e_send.at[0], e_recv.at[0], on_dp(mate))
    last.start()
    remote(fin.at[core], fin.at[1 - core], e_send.at[0], e_recv.at[0], on_dp(mate)).wait_recv()
    for h in range(2):
        chosen = jnp.where(core == 0, fin[h, :, :64], fin[h, :, 64:])
        out_out[h * H : (h + 1) * H, :] = chosen[:H]
        out_in[h * H : (h + 1) * H, :] = chosen[H:]

    last.wait_send()
    for copy in w_copies + o_copies + k_copies + m_copies + a_copies + c_copies:
        copy.wait_send()
    for q in range(NY):
        for i in range(1, S):
            j, copy = section_copy(i, q)

            @pl.when(fills(me, j))
            def _():
                copy.wait_send()
        mirror_copy(q).wait_send()
        for i in range(1, NZ):
            z_copy(i, q).wait_send()

        @pl.when(yh != q)
        def _():
            y_copy(q).wait_send()


def on_device(rings, saved, top_grad, gains, adapter_in, adapter_out):
    S = lax.axis_size("section")
    NY, NZ = rings
    _, _, T, D = saved.shape
    R = adapter_in.shape[3]
    NL, H, Q, N = S * R, R // 2, T // S, S * (R // 2) + R
    dma = pltpu.SemaphoreType.DMA
    scratch = [
        pltpu.VMEM((2 * T, D), BF16),
        pltpu.VMEM((2 * T, D), BF16),
        pltpu.VMEM((2 * T, D), BF16),
        pltpu.VMEM((2, D), F32),
        pltpu.VMEM((2, R, D), BF16),
        pltpu.VMEM((2, R, D), BF16),
        pltpu.VMEM((S, R, D), BF16),
        pltpu.VMEM((2 * T, 128), F32),
        pltpu.VMEM((T, NL + 4 * R), F32),
        pltpu.VMEM((R, NL), BF16),
        pltpu.VMEM((S, Q, NL + 4 * R), F32),
        pltpu.VMEM((S, R, NL), BF16),
        pltpu.VMEM((S, Q, 2 * NL + 2 * R), BF16),
        pltpu.VMEM((S, Q, 2 * NL + 2 * R), BF16),
        pltpu.VMEM((2, N, D), BF16),
        pltpu.VMEM((N, D), BF16),
        pltpu.VMEM((N, D), BF16),
        pltpu.VMEM((S, H, D), BF16),
        pltpu.VMEM((H, D), BF16),
        pltpu.VMEM((R, D), BF16),
        pltpu.VMEM((NZ, R, NY * 128), BF16),
        pltpu.VMEM((NY, R, 128), F32),
        pltpu.VMEM((NY, R, 128), F32),
        pltpu.VMEM((2, R, 128), F32),
        dma((7,)),
    ]
    scratch += [dma((S,))] * 10
    scratch += [dma((NY,))] * 2
    scratch += [dma((S, NY))] * 2
    scratch += [dma((NY,))] * 2
    scratch += [dma((NZ, NY))] * 2
    scratch += [dma((NY,))] * 2
    scratch += [dma((1,))] * 2
    half = D // (NY * NZ * CORES)
    shape = jax.ShapeDtypeStruct((R, half), F32)
    grad_in, grad_out = pl.pallas_call(
        partial(kernel, (S, NY, NZ, T, D, R)),
        out_shape=(shape, shape),
        in_specs=[pl.BlockSpec(memory_space=pl.ANY)] * 5,
        out_specs=(pl.BlockSpec(memory_space=pltpu.VMEM),) * 2,
        scratch_shapes=scratch,
        compiler_params=pltpu.CompilerParams(
            collective_id=0, has_side_effects=True, vmem_limit_bytes=56 * 2**20
        ),
        cost_estimate=pl.CostEstimate(
            flops=4 * 10**9, bytes_accessed=6 * 2**20, transcendentals=2 * T * R
        ),
    )(saved, top_grad, gains, jnp.swapaxes(adapter_in, 2, 3), adapter_out)
    return (grad_in.T[None], grad_out[None])


def solution(mesh):
    in_specs = (
        P("section", None, "dp", None),
        P(None, "dp", None),
        P("section", None, None),
        P("section", None, None, None),
        P("section", None, None, None),
    )
    out_specs = (P("section", "dp", None), P("section", None, "dp"))
    return jax.shard_map(
        partial(on_device, RINGS[mesh.shape["dp"]]),
        mesh=mesh, in_specs=in_specs, out_specs=out_specs, check_vma=False,
    )
```

```python
from functools import partial

import jax
import jax.numpy as jnp
from jax import lax
from jax.experimental import pallas as pl
from jax.experimental.pallas import tpu as pltpu
from jax.sharding import PartitionSpec as P

EPS = 1e-05
CORES = 2
RINGS = {64: (4, 8), 8: (2, 2), 4: (1, 2)}
BF16 = jnp.bfloat16
F32 = jnp.float32


def over_last(a, b):
    return lax.dot_general(a, b, (((1,), (1,)), ((), ())), preferred_element_type=F32)


def dot(a, b):
    return jnp.dot(a, b, preferred_element_type=F32)


def kernel(
    dims, saved, top, gains, win, wout, out,
    lhs, tv, hv, gv, iv, ov, wall, scale_v, scale_t, pre_v, pre_t, mix, early, late, coup, egot, lgot, cgot,
    act_t, low, same, ans, back, own_s, own_r, ds, dr, es, pe, ss, yb, xs, xr, fr, zs, zr, zt, yr,
    load_sem, wx_send, wx_recv, wd_send, wd_recv, wy_send, wy_recv, wc_send, wc_recv,
    e_send, e_recv, t_send, t_recv, g_send, g_recv, v_send, v_recv, k_send, k_recv,
    a_send, a_recv, o_send, o_recv, d_send, d_recv, c_send, c_recv, ty_send, ty_recv, tx_send, tx_recv, f_send, f_recv,
    z_send, z_recv, y_send, y_recv,
):
    S, NY, NZ, T, D, R = dims
    X = S // 2
    NL = S * R
    H = R // 2
    Q = T // S
    CH = D // NY
    me = lax.axis_index("section")
    dp = lax.axis_index("dp")
    x = me // 2
    yl = lax.rem(me, 2)
    core = lax.rem(dp, CORES)
    z = lax.rem(dp // CORES, NZ)
    yh = dp // (CORES * NZ)
    mate = dp + 1 - 2 * core
    mirror = S - 1 - me
    far = lax.rem(yh + 2 * yl + NY - 1, NY)
    NEAR = 128 * (3 * CH // 1024) if CH >= 1024 else CH // 2
    beside = 2 * x + 1 - yl

    def on_section(j):
        return {"section": j, "dp": dp}

    def on_dp(k):
        return {"section": me, "dp": k}

    def place(h, k, c=None):
        return h * (NZ * CORES) + k * CORES + (core if c is None else c)

    def y_next(way):
        return {"section": beside, "dp": dp if way == 0 else place(far, z)}

    def side(q, way):
        return pl.ds(q * CH, NEAR) if way == 0 else pl.ds(q * CH + NEAR, CH - NEAR)

    def peer(i):
        return lax.rem(me + i, S)

    def x_peer(i):
        return lax.rem(x + i, X)

    def in_row(k):
        return on_section(2 * k + yl)

    def remote(src, dst, send, recv, device):
        return pltpu.make_async_remote_copy(
            src_ref=src, dst_ref=dst, send_sem=send, recv_sem=recv,
            device_id=device, device_id_type=pl.DeviceIdType.MESH,
        )

    sent = []

    def go(copy):
        copy.start()
        sent.append(copy)

    def chunk(q):
        return pl.ds(q * CH, CH)

    half = pl.ds(pl.multiple_of(core * H, H), H)
    other_half = pl.ds(pl.multiple_of((1 - core) * H, H), H)
    steps_of = [(0, 1)] + [(dx, dy) for dx in sorted(range(1, X), key=lambda n: min(n, X - n)) for dy in range(2)]

    def section_at(dx, dy, sign=1):
        return 2 * lax.rem(x + X + sign * dx, X) + (1 - yl if dy else yl)

    own_unit = pltpu.make_async_copy(wout.at[0, yl, half], wall.at[x, yl, half], load_sem.at[7])
    own_unit.start()

    loads = []
    for r in range(2):
        rows = pl.ds(r * T, T)
        loads.append(pltpu.make_async_copy(saved.at[0, r], lhs.at[rows], load_sem.at[r]))
    loads.append(pltpu.make_async_copy(gains.at[0], gv, load_sem.at[2]))
    loads.append(pltpu.make_async_copy(win.at[0], iv, load_sem.at[3]))
    loads.append(pltpu.make_async_copy(wout.at[0], ov, load_sem.at[4]))
    for r in range(2):
        rows = pl.ds(r * T, T)
        loads.append(pltpu.make_async_copy(top.at[r], tv.at[rows], load_sem.at[5 + r]))
    for copy in loads:
        copy.start()

    barrier = pltpu.get_barrier_semaphore()
    greeted = [on_section(peer(i)) for i in range(1, S)] + [on_dp(mate)]
    greeted += [{"section": beside, "dp": place(far, z)}]
    greeted += [on_dp(place(yh, lax.rem(z + i, NZ))) for i in range(1, NZ)]
    greeted += [on_dp(place(lax.rem(yh + i, NY), z, c)) for i in range(1, NY) for c in range(CORES)]
    for device in greeted:
        pl.semaphore_signal(barrier, inc=1, device_id=device, device_id_type=pl.DeviceIdType.MESH)
    pl.semaphore_wait(barrier, len(greeted))

    near = pl.ds(0, D // 2)
    rest = pl.ds(D // 2, D // 2)

    def upper(j):
        return jnp.where(j > me, 0, 1)

    rows_sent = []
    for i in range(1, X):
        j = 2 * x_peer(i) + yl
        copy = remote(
            wout.at[0, upper(j), half, near], wall.at[x, yl, half, near], wx_send.at[i], wx_recv.at[x], on_section(j)
        )
        copy.start()
        rows_sent.append(copy)

    def send_direct():
        for copy in rows_sent:
            copy.wait_send()
        for n, (dx, dy) in reversed(list(enumerate(steps_of))):
            j = section_at(dx, dy)
            go(remote(
                wout.at[0, upper(j), half, rest], wall.at[x, yl, half, rest],
                wd_send.at[n], wd_recv.at[me], on_section(j),
            ))

    for j in range(S):
        @pl.when(j >= me)
        def _():
            low[j * R : (j + 1) * R, 0:T] = jnp.zeros((R, T), BF16)

        @pl.when(j >= mirror)
        def _():
            low[j * R : (j + 1) * R, T : 2 * T] = jnp.zeros((R, T), BF16)

    xr[x] = jnp.zeros((H, D), BF16)

    def onward(way):
        return pl.ds(way * (D // 4), D // 4)

    def gather_row():
        own_unit.wait()
        for i in range(1, X):
            k = x_peer(X - i)
            landed = wall.at[k, yl, half, near]
            remote(landed, landed, wx_send.at[i], wx_recv.at[k], in_row(k)).wait_recv()
        for way in range(2):
            row = wall.at[:, yl, half, onward(way)]
            go(remote(row, row, wy_send.at[way], wy_recv.at[way], y_next(way)))
        row = wall.at[:, yl, half, near]
        go(remote(row, row, wc_send.at[0], wc_recv.at[0], on_dp(mate)))

    def gather_y():
        for way in range(2):
            row = wall.at[:, 1 - yl, half, onward(way)]
            remote(row, row, wy_send.at[way], wy_recv.at[way], y_next(way)).wait_recv()
        row = wall.at[:, 1 - yl, half, near]
        go(remote(row, row, wc_send.at[1], wc_recv.at[1], on_dp(mate)))

    def gather_direct():
        for n, (dx, dy) in enumerate(steps_of):
            j = section_at(dx, dy, -1)
            landed = wall.at[j // 2, lax.rem(j, 2), half, rest]
            remote(landed, landed, wd_send.at[n], wd_recv.at[j], on_section(j)).wait_recv()
        row = wall.at[:, :, half, rest]
        go(remote(row, row, wc_send.at[2], wc_recv.at[2], on_dp(mate)))

    def project_near():
        for n, line in enumerate((yl, 1 - yl)):
            row = wall.at[:, line, other_half, near]
            remote(row, row, wc_send.at[n], wc_recv.at[n], on_dp(mate)).wait_recv()
        return over_last(lhs[:, : D // 2], wall[:, :, :, : D // 2].reshape(NL, D // 2))

    def project_rest():
        row = wall.at[:, :, other_half, rest]
        remote(row, row, wc_send.at[2], wc_recv.at[2], on_dp(mate)).wait_recv()
        return over_last(lhs[:, D // 2 :], wall[:, :, :, D // 2 :].reshape(NL, D // 2))

    def piece_norm():
        for n in range(2):
            loads[n].wait()

        def squares(i, acc):
            xf = lhs[0 : 2 * T, pl.ds(pl.multiple_of(i * 128, 128), 128)].astype(F32)
            return acc + xf * xf

        total = lax.fori_loop(0, D // 128, squares, jnp.zeros((2 * T, 128), F32), unroll=2)
        scale = lax.rsqrt(jnp.sum(total, axis=-1, keepdims=True) * (1.0 / D) + EPS)
        wide = jnp.broadcast_to(scale, (2 * T, 128))
        scale_v[...] = wide
        scale_t[...] = wide.T[0:8]

    def piece_hidden():
        for n in range(2, 5):
            loads[n].wait()

        def normed(i, carry):
            cols = pl.ds(pl.multiple_of(i * 128, 128), 128)
            for r in range(2):
                rows = slice(r * T, (r + 1) * T)
                nf = lhs[rows, cols].astype(F32) * scale_v[rows, :]
                hv[rows, cols] = (nf * gv[r : r + 1, cols]).astype(BF16)
                lhs[2 * T + r * R : 2 * T + (r + 1) * R, cols] = (
                    iv[r, :, cols].astype(F32) * gv[r : r + 1, cols]
                ).astype(BF16)
            return carry

        lax.fori_loop(0, D // 128, normed, 0)

    def piece_down():
        for r in range(2):
            rows = slice(r * T, (r + 1) * T)
            pre = over_last(hv[rows, :], iv[r])
            pre_v[:, r * R : (r + 1) * R] = pre
            early[:, r * R : (r + 1) * R] = pre
        pre = pre_v[...].T
        pre_t[...] = pre
        active = pre * jax.nn.sigmoid(pre)
        for r in range(2):
            act_t[r] = active[r * R : (r + 1) * R].astype(BF16)
        same[:, 0:T] = act_t[0]
        for i in range(1, S):
            j = peer(i)
            replica = jnp.where(j > me, 0, 1)
            rows = pl.ds(pl.multiple_of(jnp.where(j > me, me, mirror) * R, R), R)
            lanes = pl.ds(pl.multiple_of(replica * T, T), T)
            go(remote(act_t.at[replica], low.at[rows, lanes], t_send.at[i], t_recv.at[me], on_section(j)))
        go(remote(act_t.at[1], same.at[:, pl.ds(T, T)], g_send.at[0], g_recv.at[0], on_section(mirror)))

    def piece_up():
        for n in range(5, 7):
            loads[n].wait()
        for r in range(2):
            rows = slice(r * T, (r + 1) * T)
            early[:, (2 + r) * R : (3 + r) * R] = over_last(tv[rows, :], ov[r])
        for i in range(1, S):
            j = peer(i)
            rows = pl.ds(pl.multiple_of(j * Q, Q), Q)
            go(remote(early.at[rows], egot.at[me], e_send.at[i], e_recv.at[me], on_section(j)))
        egot[me] = early[pl.ds(pl.multiple_of(me * Q, Q), Q), :]

    piece_norm()
    send_direct()
    piece_hidden()
    gather_row()
    piece_down()
    piece_up()
    gather_y()
    gather_direct()
    across = project_near() + project_rest()

    block = lax.broadcasted_iota(jnp.int32, (R, NL), 1) // R
    coup[...] = jnp.where(
        block < me, across[2 * T : 2 * T + R], across[2 * T + R :]
    ).astype(BF16)
    lane = lax.broadcasted_iota(jnp.int32, (T, NL), 1)
    block = lane // R
    within = lax.rem(lane, R) // (R // 4)
    sc0 = scale_v[:T, 0:1]
    sc1 = scale_v[T:, 0:1]
    sc = jnp.where(within < 2, sc0, sc1)
    rounded = sc.astype(BF16).astype(F32)
    own = jnp.where(lax.rem(within, 2) == 0, rounded, sc - rounded)
    late[...] = jnp.where(
        block < me, across[:T] * (sc0 * sc0), jnp.where(block > me, across[T : 2 * T] * (sc1 * sc1), own)
    ).astype(BF16)
    for i in range(1, S):
        j = peer(i)
        rows = pl.ds(pl.multiple_of(j * Q, Q), Q)
        go(remote(coup, cgot.at[me], k_send.at[i], k_recv.at[me], on_section(j)))
        go(remote(late.at[rows], lgot.at[me], v_send.at[i], v_recv.at[me], on_section(j)))
    cgot[me] = coup[...]
    lgot[me] = late[pl.ds(pl.multiple_of(me * Q, Q), Q), :]

    remote(act_t.at[1], same.at[:, pl.ds(T, T)], g_send.at[0], g_recv.at[0], on_section(mirror)).wait_recv()
    for q in range(NY):
        term = dot(same[...], tv[:, chunk(q)])
        for h in range(2):
            own_s[h, :, chunk(q)] = term[h * H : (h + 1) * H]
    go(remote(own_s.at[1 - core], own_r, o_send.at[0], o_recv.at[0], on_dp(mate)))

    for i in range(1, S):
        j = peer(S - i)
        remote(early.at[pl.ds(0, Q)], egot.at[j], e_send.at[i], e_recv.at[j], on_section(j)).wait_recv()
    pre = egot[:, :, 0 : 2 * R]
    sig = jax.nn.sigmoid(pre)
    slope = sig * (1.0 + pre * (1.0 - sig))
    for i in range(1, S):
        j = peer(S - i)
        remote(coup, cgot.at[j], k_send.at[i], k_recv.at[j], on_section(j)).wait_recv()
        remote(late.at[pl.ds(0, Q)], lgot.at[j], v_send.at[i], v_recv.at[j], on_section(j)).wait_recv()

    acc = [jnp.zeros((Q, NL), F32), jnp.zeros((Q, NL), F32)]
    for turn in range(S):
        for r in range(2):
            k = S - 1 - turn if r == 0 else turn
            lanes = slice(r * R, (r + 1) * R)
            up = egot[k, :, (2 + r) * R : (3 + r) * R]
            if turn > 0:
                up = up + acc[r][:, k * R : (k + 1) * R]
            delta = (up * slope[k, :, lanes]).astype(BF16)
            ans[k, :, lanes] = delta
            if turn < S - 1:
                inner = jnp.sum(delta.astype(F32) * pre[k, :, lanes], axis=-1, keepdims=True) * (1.0 / D)
                first = k * R + r * H
                sc = lgot[k, :, first : first + 1].astype(F32)
                sc = sc + lgot[k, :, first + R // 4 : first + R // 4 + 1].astype(F32)
                acc[r] = acc[r] + sc * dot(delta, cgot[k]) - inner * lgot[k].astype(F32)
    for i in range(1, S):
        j = peer(i)
        go(remote(ans.at[j], back.at[me], a_send.at[i], a_recv.at[me], on_section(j)))
    back[me] = ans[me]
    for i in range(1, S):
        j = peer(S - i)
        rows = pl.ds(pl.multiple_of(jnp.where(j < me, j, S - 1 - j) * R, R), R)
        lanes = pl.ds(pl.multiple_of(jnp.where(j < me, 0, T), T), T)
        remote(act_t.at[0], low.at[rows, lanes], t_send.at[i], t_recv.at[j], on_section(j)).wait_recv()
    lower = low[...].astype(F32)
    for i in range(1, S):
        j = peer(S - i)
        remote(ans.at[j], back.at[j], a_send.at[i], a_recv.at[j], on_section(j)).wait_recv()

    answer = back[...].reshape(T, 128)
    deltas = [answer[:, r * R : (r + 1) * R] for r in range(2)]
    turned = answer[:, 0 : 2 * R].astype(F32).T.astype(BF16)
    for r in range(2):
        tokens = slice(r * T, (r + 1) * T)
        seen = lower[:, tokens]
        tall = turned[r * R : (r + 1) * R].astype(F32) * pre_t[r * R : (r + 1) * R]
        sc = scale_t[0:1, tokens]
        pull = jnp.sum(tall, axis=0, keepdims=True) * (-1.0 / D) * (sc * sc)
        mix[:, tokens] = (seen * pull).astype(BF16)
        scaled = (deltas[r].astype(F32) * scale_v[tokens, 0:1]).astype(BF16)
        mix[:, 2 * T + r * R : 2 * T + (r + 1) * R] = dot(low[:, tokens], scaled).astype(BF16)
    W = min(512, CH)

    def terms(q):
        def part(i, carry):
            cols = pl.ds(pl.multiple_of(q * CH + i * W, W), W)
            below = dot(mix[...], lhs[:, cols]).astype(BF16)
            for j in range(S):
                for h in range(2):
                    es[h, j // 2, j % 2, :, cols] = below[j * R + h * H : j * R + (h + 1) * H]
            return carry

        lax.fori_loop(0, CH // W, part, 0)
        go(remote(
            es.at[1 - core, :, :, :, chunk(q)], pe.at[:, :, :, chunk(q)],
            c_send.at[q], c_recv.at[q], on_dp(mate),
        ))

    def down_terms(q):
        def part(i, carry):
            cols = pl.ds(pl.multiple_of(i * W, W), W)
            for r in range(2):
                rows = slice(r * T, (r + 1) * T)
                term = dot(turned[r * R : (r + 1) * R], hv[rows, cols]).astype(BF16)
                for h in range(2):
                    ds[h, r, :, cols] = term[h * H : (h + 1) * H]
            return carry

        lax.fori_loop(0, D // W, part, 0)
        go(remote(ds.at[1 - core], dr, d_send.at[0], d_recv.at[0], on_dp(mate)))

    def down_send(q):
        remote(dr, dr, d_send.at[0], d_recv.at[0], on_dp(mate)).wait_recv()
        dr[...] = (ds[core].astype(F32) + dr[...].astype(F32)).astype(BF16)
        go(remote(dr.at[1], fr, f_send.at[0], f_recv.at[0], on_section(mirror)))

    def step_y(q):
        landed = pe.at[:, :, :, chunk(q)]
        remote(landed, landed, c_send.at[q], c_recv.at[q], on_dp(mate)).wait_recv()
        ss[:, :, :, chunk(q)] = (
            es[core, :, :, :, chunk(q)].astype(F32) + pe[:, :, :, chunk(q)].astype(F32)
        ).astype(BF16)
        for way in range(2):
            go(remote(
                ss.at[:, 1 - yl, :, side(q, way)], yb.at[:, :, side(q, way)],
                ty_send.at[way, q], ty_recv.at[way, q], y_next(way),
            ))

    def step_x(q):
        for way in range(2):
            landed = yb.at[:, :, side(q, way)]
            remote(landed, landed, ty_send.at[way, q], ty_recv.at[way, q], y_next(way)).wait_recv()
        xs[:, :, chunk(q)] = (
            ss[:, yl, :, chunk(q)].astype(F32) + yb[:, :, chunk(q)].astype(F32)
        ).astype(BF16)
        for i in range(1, X):
            k = x_peer(i)
            go(remote(xs.at[k, :, chunk(q)], xr.at[x, :, chunk(q)], tx_send.at[i, q], tx_recv.at[x, q], in_row(k)))

    def step_z(q):
        for i in range(1, X):
            k = x_peer(X - i)
            landed = xr.at[k, :, chunk(q)]
            remote(landed, landed, tx_send.at[i, q], tx_recv.at[k, q], in_row(k)).wait_recv()
        if q == 0:
            remote(fr, fr, f_send.at[0], f_recv.at[0], on_section(mirror)).wait_recv()
            remote(own_r, own_r, o_send.at[0], o_recv.at[0], on_dp(mate)).wait_recv()
        whole = own_s[core, :, chunk(q)] + own_r[:, chunk(q)] + xs[x, :, chunk(q)].astype(F32)
        for k in range(X):
            whole = whole + xr[k, :, chunk(q)].astype(F32)
        zs[0:H, chunk(q)] = whole.astype(BF16)
        zs[H:R, chunk(q)] = (dr[0, :, chunk(q)].astype(F32) + fr[:, chunk(q)].astype(F32)).astype(BF16)
        for i in range(1, NZ):
            k = lax.rem(z + i, NZ)
            source = pl.ds(pl.multiple_of(q * CH + k * 128, 128), 128)
            go(remote(
                zs.at[:, source], zr.at[z, :, pl.ds(q * 128, 128)],
                z_send.at[i, q], z_recv.at[z, q], on_dp(place(yh, k)),
            ))
        zr[z, :, q * 128 : (q + 1) * 128] = zs[:, pl.ds(pl.multiple_of(q * CH + z * 128, 128), 128)]

    def y_copy(q, c):
        return remote(
            zt.at[q], yr.at[core, yh], y_send.at[c, q], y_recv.at[core, yh], on_dp(place(q, z, c))
        )

    def on_other(q, c, act):
        @pl.when((yh != q) | (core != c))
        def _():
            act()

    def step_yh(q):
        for i in range(1, NZ):
            k = lax.rem(z + NZ - i, NZ)
            landed = zr.at[k, :, pl.ds(q * 128, 128)]
            remote(landed, landed, z_send.at[i, q], z_recv.at[k, q], on_dp(place(yh, k))).wait_recv()
        whole = zr[0, :, q * 128 : (q + 1) * 128].astype(F32)
        for k in range(1, NZ):
            whole = whole + zr[k, :, q * 128 : (q + 1) * 128].astype(F32)
        zt[q] = whole

        for c in range(CORES):
            on_other(q, c, lambda: y_copy(q, c).start())

        @pl.when(yh == q)
        def _():
            yr[core, q] = zt[q]

    steps = [(terms, 0.0), (step_y, 1.1), (step_x, 3.4), (step_z, 5.6), (step_yh, 7.8)]
    order = [(q + late_by, step, q) for step, late_by in steps for q in range(NY)]
    order += [(1.3, down_terms, 0), (2.1, down_send, 0)]
    for _, step, q in sorted(order, key=lambda entry: entry[0]):
        step(q)

    for c in range(CORES):
        for k in range(NY):
            landed = yr.at[c, k]
            copy = remote(landed, landed, y_send.at[c, k], y_recv.at[c, k], on_dp(place(k, z, c)))
            on_other(k, c, copy.wait_recv)
    for c in range(CORES):
        whole = yr[c, 0]
        for k in range(1, NY):
            whole = whole + yr[c, k]
        out[c] = whole

    for copy in sent:
        copy.wait_send()
    for q in range(NY):
        for c in range(CORES):
            on_other(q, c, y_copy(q, c).wait_send)


def own_columns(parts, out_in, out_out):
    core = lax.rem(lax.axis_index("dp"), CORES)
    H = parts.shape[1] // 2
    for h in range(2):
        chosen = jnp.where(core == 0, parts[h, :, :64], parts[h, :, 64:])
        out_out[h * H : (h + 1) * H, :] = chosen[:H]
        out_in[h * H : (h + 1) * H, :] = chosen[H:]


def on_device(rings, saved, top_grad, gains, adapter_in, adapter_out):
    S = lax.axis_size("section")
    NY, NZ = rings
    _, _, T, D = saved.shape
    R = adapter_in.shape[3]
    X, NL, H, Q = S // 2, S * R, R // 2, T // S
    dma = pltpu.SemaphoreType.DMA
    scratch = [
        pltpu.VMEM((2 * T + 2 * R, D), BF16),
        pltpu.VMEM((2 * T, D), BF16),
        pltpu.VMEM((2 * T, D), BF16),
        pltpu.VMEM((2, D), F32),
        pltpu.VMEM((2, R, D), BF16),
        pltpu.VMEM((2, R, D), BF16),
        pltpu.VMEM((X, 2, R, D), BF16),
        pltpu.VMEM((2 * T, 128), F32),
        pltpu.VMEM((8, 2 * T), F32),
        pltpu.VMEM((T, 2 * R), F32),
        pltpu.VMEM((2 * R, T), F32),
        pltpu.VMEM((NL, 2 * T + 2 * R), BF16),
        pltpu.VMEM((T, 4 * R), F32),
        pltpu.VMEM((T, NL), BF16),
        pltpu.VMEM((R, NL), BF16),
        pltpu.VMEM((S, Q, 4 * R), F32),
        pltpu.VMEM((S, Q, NL), BF16),
        pltpu.VMEM((S, R, NL), BF16),
        pltpu.VMEM((2, R, T), BF16),
        pltpu.VMEM((NL, 2 * T), BF16),
        pltpu.VMEM((R, 2 * T), BF16),
        pltpu.VMEM((S, Q, 128), BF16),
        pltpu.VMEM((S, Q, 128), BF16),
        pltpu.VMEM((2, H, D), F32),
        pltpu.VMEM((H, D), F32),
        pltpu.VMEM((2, 2, H, D), BF16),
        pltpu.VMEM((2, H, D), BF16),
        pltpu.VMEM((2, X, 2, H, D), BF16),
        pltpu.VMEM((X, 2, H, D), BF16),
        pltpu.VMEM((X, 2, H, D), BF16),
        pltpu.VMEM((X, H, D), BF16),
        pltpu.VMEM((X, H, D), BF16),
        pltpu.VMEM((X, H, D), BF16),
        pltpu.VMEM((H, D), BF16),
        pltpu.VMEM((R, D), BF16),
        pltpu.VMEM((NZ, R, NY * 128), BF16),
        pltpu.VMEM((NY, R, 128), F32),
        pltpu.VMEM((CORES, NY, R, 128), F32),
        dma((8,)),
    ]
    scratch += [dma((X,))] * 2 + [dma((S,))] * 2 + [dma((2,))] * 2 + [dma((3,))] * 2
    scratch += [dma((S,))] * 4 + [dma((1,))] * 2 + [dma((S,))] * 4
    scratch += [dma((S,))] * 2 + [dma((1,))] * 4 + [dma((NY,))] * 2 + [dma((2, NY))] * 2
    scratch += [dma((X, NY))] * 2 + [dma((1,))] * 2
    scratch += [dma((NZ, NY))] * 2 + [dma((CORES, NY))] * 2
    half = D // (NY * NZ * CORES)
    vmem = pl.BlockSpec(memory_space=pltpu.VMEM)
    parts = pl.pallas_call(
        partial(kernel, (S, NY, NZ, T, D, R)),
        out_shape=jax.ShapeDtypeStruct((2, R, 128), F32),
        in_specs=[pl.BlockSpec(memory_space=pl.ANY)] * 5,
        out_specs=vmem,
        scratch_shapes=scratch,
        compiler_params=pltpu.CompilerParams(
            collective_id=0, has_side_effects=True, vmem_limit_bytes=56 * 2**20
        ),
        cost_estimate=pl.CostEstimate(
            flops=4 * 10**9, bytes_accessed=6 * 2**20, transcendentals=2 * T * R
        ),
    )(saved, top_grad, gains, jnp.swapaxes(adapter_in, 2, 3), adapter_out)
    shape = jax.ShapeDtypeStruct((R, half), F32)
    grad_in, grad_out = pl.pallas_call(
        own_columns, out_shape=(shape, shape), in_specs=[vmem], out_specs=(vmem, vmem)
    )(parts)
    return (grad_in.T[None], grad_out[None])


def solution(mesh):
    in_specs = (
        P("section", None, "dp", None),
        P(None, "dp", None),
        P("section", None, None),
        P("section", None, None, None),
        P("section", None, None, None),
    )
    out_specs = (P("section", "dp", None), P("section", None, "dp"))
    return jax.shard_map(
        partial(on_device, RINGS[mesh.shape["dp"]]),
        mesh=mesh, in_specs=in_specs, out_specs=out_specs, check_vma=False,
    )
```

```python
from functools import partial

import jax
import jax.numpy as jnp
from jax import lax
from jax.experimental import pallas as pl
from jax.experimental.pallas import tpu as pltpu
from jax.sharding import PartitionSpec as P

EPS = 1e-05
CORES = 2
RINGS = {64: (4, 8), 8: (2, 2), 4: (1, 2)}
BF16 = jnp.bfloat16
F32 = jnp.float32


def over_last(a, b):
    return lax.dot_general(a, b, (((1,), (1,)), ((), ())), preferred_element_type=F32)


def dot(a, b):
    return jnp.dot(a, b, preferred_element_type=F32)


def kernel(
    dims, saved, top, gains, win, wout, out,
    lhs, tv, hv, gv, iv, ov, wall, scale_v, scale_t, pre_v, pre_t, mix, early, late, coup, egot, lgot, cgot,
    act_t, low, same, ans, back, own_s, own_r, ds, dr, es, pe, ss, yb, xs, xr, fr, zs, zr, zt, yr,
    load_sem, wx_send, wx_recv, wd_send, wd_recv, wy_send, wy_recv, wz_send, wz_recv, wc_send, wc_recv,
    e_send, e_recv, t_send, t_recv, g_send, g_recv, v_send, v_recv, k_send, k_recv,
    a_send, a_recv, o_send, o_recv, d_send, d_recv, c_send, c_recv, ty_send, ty_recv, tx_send, tx_recv, f_send, f_recv,
    z_send, z_recv, y_send, y_recv,
):
    S, NY, NZ, T, D, R = dims
    X = S // 2
    NL = S * R
    H = R // 2
    Q = T // S
    CH = D // NY
    me = lax.axis_index("section")
    dp = lax.axis_index("dp")
    x = me // 2
    yl = lax.rem(me, 2)
    core = lax.rem(dp, CORES)
    z = lax.rem(dp // CORES, NZ)
    yh = dp // (CORES * NZ)
    mate = dp + 1 - 2 * core
    mirror = S - 1 - me
    far = lax.rem(yh + 2 * yl + NY - 1, NY)
    NEAR = 128 * (3 * CH // 1024) if CH >= 1024 else CH // 2
    beside = 2 * x + 1 - yl

    def on_section(j):
        return {"section": j, "dp": dp}

    def on_dp(k):
        return {"section": me, "dp": k}

    def place(h, k, c=None):
        return h * (NZ * CORES) + k * CORES + (core if c is None else c)

    def y_next(way):
        return {"section": beside, "dp": dp if way == 0 else place(far, z)}

    def side(q, way):
        return pl.ds(q * CH, NEAR) if way == 0 else pl.ds(q * CH + NEAR, CH - NEAR)

    def peer(i):
        return lax.rem(me + i, S)

    def x_peer(i):
        return lax.rem(x + i, X)

    def in_row(k):
        return on_section(2 * k + yl)

    def remote(src, dst, send, recv, device):
        return pltpu.make_async_remote_copy(
            src_ref=src, dst_ref=dst, send_sem=send, recv_sem=recv,
            device_id=device, device_id_type=pl.DeviceIdType.MESH,
        )

    sent = []

    def go(copy):
        copy.start()
        sent.append(copy)

    def chunk(q):
        return pl.ds(q * CH, CH)

    half = pl.ds(pl.multiple_of(core * H, H), H)
    other_half = pl.ds(pl.multiple_of((1 - core) * H, H), H)
    steps_of = [(0, 1)] + [(dx, dy) for dx in sorted(range(1, X), key=lambda n: min(n, X - n)) for dy in range(2)]

    def section_at(dx, dy, sign=1):
        return 2 * lax.rem(x + X + sign * dx, X) + (1 - yl if dy else yl)

    near = pl.ds(0, D // 2)
    E = D // 4
    odd = lax.rem(z, 2)
    mine_z = pl.ds(pl.multiple_of(D // 2 + odd * E, E), E)
    theirs_z = pl.ds(pl.multiple_of(D // 2 + (1 - odd) * E, E), E)
    own_units = [
        pltpu.make_async_copy(wout.at[0, yl, half, cols], wall.at[x, yl, half, cols], load_sem.at[7 + n])
        for n, cols in enumerate((near, mine_z))
    ]
    for copy in own_units:
        copy.start()

    loads = []
    for r in range(2):
        rows = pl.ds(r * T, T)
        loads.append(pltpu.make_async_copy(saved.at[0, r], lhs.at[rows], load_sem.at[r]))
    loads.append(pltpu.make_async_copy(gains.at[0], gv, load_sem.at[2]))
    loads.append(pltpu.make_async_copy(win.at[0], iv, load_sem.at[3]))
    loads.append(pltpu.make_async_copy(wout.at[0], ov, load_sem.at[4]))
    for r in range(2):
        rows = pl.ds(r * T, T)
        loads.append(pltpu.make_async_copy(top.at[r], tv.at[rows], load_sem.at[5 + r]))
    for copy in loads:
        copy.start()

    barrier = pltpu.get_barrier_semaphore()
    greeted = [on_section(peer(i)) for i in range(1, S)] + [on_dp(mate)]
    greeted += [{"section": beside, "dp": place(far, z)}]
    greeted += [on_dp(place(yh, lax.rem(z + i, NZ))) for i in range(1, NZ)]
    greeted += [on_dp(place(lax.rem(yh + i, NY), z, c)) for i in range(1, NY) for c in range(CORES)]
    for device in greeted:
        pl.semaphore_signal(barrier, inc=1, device_id=device, device_id_type=pl.DeviceIdType.MESH)
    pl.semaphore_wait(barrier, len(greeted))

    def upper(j):
        return jnp.where(j > me, 0, 1)

    for i in range(1, X):
        j = 2 * x_peer(i) + yl
        go(remote(
            wout.at[0, upper(j), half, near], wall.at[x, yl, half, near], wx_send.at[i], wx_recv.at[x], on_section(j)
        ))
    for n, (dx, dy) in reversed(list(enumerate(steps_of))):
        j = section_at(dx, dy)
        go(remote(
            wout.at[0, upper(j), half, mine_z], wall.at[x, yl, half, mine_z],
            wd_send.at[n], wd_recv.at[me], on_section(j),
        ))

    for j in range(S):
        @pl.when(j >= me)
        def _():
            low[j * R : (j + 1) * R, 0:T] = jnp.zeros((R, T), BF16)

        @pl.when(j >= mirror)
        def _():
            low[j * R : (j + 1) * R, T : 2 * T] = jnp.zeros((R, T), BF16)

    xr[x] = jnp.zeros((H, D), BF16)

    def onward(way):
        return pl.ds(way * E, E)

    def onward_z(way, parity):
        return pl.ds(pl.multiple_of(D // 2 + parity * E + way * (E // 2), E // 2), E // 2)

    def z_next(way):
        return on_dp(place(yh, lax.rem(z + (1 if way == 0 else NZ - 1), NZ)))

    def gather_row():
        own_units[0].wait()
        for i in range(1, X):
            k = x_peer(X - i)
            landed = wall.at[k, yl, half, near]
            remote(landed, landed, wx_send.at[i], wx_recv.at[k], in_row(k)).wait_recv()
        for way in range(2):
            row = wall.at[:, yl, half, onward(way)]
            go(remote(row, row, wy_send.at[way], wy_recv.at[way], y_next(way)))
        row = wall.at[:, yl, half, near]
        go(remote(row, row, wc_send.at[0], wc_recv.at[0], on_dp(mate)))

    def gather_direct():
        own_units[1].wait()
        for n, (dx, dy) in enumerate(steps_of):
            j = section_at(dx, dy, -1)
            landed = wall.at[j // 2, lax.rem(j, 2), half, mine_z]
            remote(landed, landed, wd_send.at[n], wd_recv.at[j], on_section(j)).wait_recv()
        for way in range(2):
            part = wall.at[:, :, half, onward_z(way, odd)]
            go(remote(part, part, wz_send.at[way], wz_recv.at[way], z_next(way)))
        part = wall.at[:, :, half, mine_z]
        go(remote(part, part, wc_send.at[1], wc_recv.at[1], on_dp(mate)))

    def gather_y():
        for way in range(2):
            row = wall.at[:, 1 - yl, half, onward(way)]
            remote(row, row, wy_send.at[way], wy_recv.at[way], y_next(way)).wait_recv()
        row = wall.at[:, 1 - yl, half, near]
        go(remote(row, row, wc_send.at[2], wc_recv.at[2], on_dp(mate)))

    def gather_z():
        for way in range(2):
            part = wall.at[:, :, half, onward_z(way, 1 - odd)]
            remote(part, part, wz_send.at[way], wz_recv.at[way], z_next(way)).wait_recv()
        part = wall.at[:, :, half, theirs_z]
        go(remote(part, part, wc_send.at[3], wc_recv.at[3], on_dp(mate)))

    def project_near():
        for n, line in ((0, yl), (2, 1 - yl)):
            row = wall.at[:, line, other_half, near]
            remote(row, row, wc_send.at[n], wc_recv.at[n], on_dp(mate)).wait_recv()
        return over_last(lhs[:, : D // 2], wall[:, :, :, : D // 2].reshape(NL, D // 2))

    def project_rest():
        for n, cols in ((1, mine_z), (3, theirs_z)):
            part = wall.at[:, :, other_half, cols]
            remote(part, part, wc_send.at[n], wc_recv.at[n], on_dp(mate)).wait_recv()
        return over_last(lhs[:, D // 2 :], wall[:, :, :, D // 2 :].reshape(NL, D // 2))

    def piece_norm():
        for n in range(2):
            loads[n].wait()

        def squares(i, acc):
            xf = lhs[0 : 2 * T, pl.ds(pl.multiple_of(i * 128, 128), 128)].astype(F32)
            return acc + xf * xf

        total = lax.fori_loop(0, D // 128, squares, jnp.zeros((2 * T, 128), F32), unroll=2)
        scale = lax.rsqrt(jnp.sum(total, axis=-1, keepdims=True) * (1.0 / D) + EPS)
        wide = jnp.broadcast_to(scale, (2 * T, 128))
        scale_v[...] = wide
        scale_t[...] = wide.T[0:8]

    def piece_hidden():
        for n in range(2, 5):
            loads[n].wait()

        def normed(i, carry):
            cols = pl.ds(pl.multiple_of(i * 128, 128), 128)
            for r in range(2):
                rows = slice(r * T, (r + 1) * T)
                nf = lhs[rows, cols].astype(F32) * scale_v[rows, :]
                hv[rows, cols] = (nf * gv[r : r + 1, cols]).astype(BF16)
                lhs[2 * T + r * R : 2 * T + (r + 1) * R, cols] = (
                    iv[r, :, cols].astype(F32) * gv[r : r + 1, cols]
                ).astype(BF16)
            return carry

        lax.fori_loop(0, D // 128, normed, 0)

    def piece_down():
        for r in range(2):
            rows = slice(r * T, (r + 1) * T)
            pre = over_last(hv[rows, :], iv[r])
            pre_v[:, r * R : (r + 1) * R] = pre
            early[:, r * R : (r + 1) * R] = pre
        pre = pre_v[...].T
        pre_t[...] = pre
        active = pre * jax.nn.sigmoid(pre)
        for r in range(2):
            act_t[r] = active[r * R : (r + 1) * R].astype(BF16)
        same[:, 0:T] = act_t[0]
        for i in range(1, S):
            j = peer(i)
            replica = jnp.where(j > me, 0, 1)
            rows = pl.ds(pl.multiple_of(jnp.where(j > me, me, mirror) * R, R), R)
            lanes = pl.ds(pl.multiple_of(replica * T, T), T)
            go(remote(act_t.at[replica], low.at[rows, lanes], t_send.at[i], t_recv.at[me], on_section(j)))
        go(remote(act_t.at[1], same.at[:, pl.ds(T, T)], g_send.at[0], g_recv.at[0], on_section(mirror)))

    def piece_up():
        for n in range(5, 7):
            loads[n].wait()
        for r in range(2):
            rows = slice(r * T, (r + 1) * T)
            early[:, (2 + r) * R : (3 + r) * R] = over_last(tv[rows, :], ov[r])
        for i in range(1, S):
            j = peer(i)
            rows = pl.ds(pl.multiple_of(j * Q, Q), Q)
            go(remote(early.at[rows], egot.at[me], e_send.at[i], e_recv.at[me], on_section(j)))
        egot[me] = early[pl.ds(pl.multiple_of(me * Q, Q), Q), :]

    piece_norm()
    piece_hidden()
    gather_row()
    gather_direct()
    piece_down()
    piece_up()
    gather_y()
    gather_z()
    across = project_near() + project_rest()

    block = lax.broadcasted_iota(jnp.int32, (R, NL), 1) // R
    coup[...] = jnp.where(
        block < me, across[2 * T : 2 * T + R], across[2 * T + R :]
    ).astype(BF16)
    lane = lax.broadcasted_iota(jnp.int32, (T, NL), 1)
    block = lane // R
    within = lax.rem(lane, R) // (R // 4)
    sc0 = scale_v[:T, 0:1]
    sc1 = scale_v[T:, 0:1]
    sc = jnp.where(within < 2, sc0, sc1)
    rounded = sc.astype(BF16).astype(F32)
    own = jnp.where(lax.rem(within, 2) == 0, rounded, sc - rounded)
    late[...] = jnp.where(
        block < me, across[:T] * (sc0 * sc0), jnp.where(block > me, across[T : 2 * T] * (sc1 * sc1), own)
    ).astype(BF16)
    for i in range(1, S):
        j = peer(i)
        rows = pl.ds(pl.multiple_of(j * Q, Q), Q)
        go(remote(coup, cgot.at[me], k_send.at[i], k_recv.at[me], on_section(j)))
        go(remote(late.at[rows], lgot.at[me], v_send.at[i], v_recv.at[me], on_section(j)))
    cgot[me] = coup[...]
    lgot[me] = late[pl.ds(pl.multiple_of(me * Q, Q), Q), :]

    remote(act_t.at[1], same.at[:, pl.ds(T, T)], g_send.at[0], g_recv.at[0], on_section(mirror)).wait_recv()
    for q in range(NY):
        term = dot(same[...], tv[:, chunk(q)])
        for h in range(2):
            own_s[h, :, chunk(q)] = term[h * H : (h + 1) * H]
    go(remote(own_s.at[1 - core], own_r, o_send.at[0], o_recv.at[0], on_dp(mate)))

    for i in range(1, S):
        j = peer(S - i)
        remote(early.at[pl.ds(0, Q)], egot.at[j], e_send.at[i], e_recv.at[j], on_section(j)).wait_recv()
    pre = egot[:, :, 0 : 2 * R]
    sig = jax.nn.sigmoid(pre)
    slope = sig * (1.0 + pre * (1.0 - sig))
    for i in range(1, S):
        j = peer(S - i)
        remote(coup, cgot.at[j], k_send.at[i], k_recv.at[j], on_section(j)).wait_recv()
        remote(late.at[pl.ds(0, Q)], lgot.at[j], v_send.at[i], v_recv.at[j], on_section(j)).wait_recv()

    acc = [jnp.zeros((Q, NL), F32), jnp.zeros((Q, NL), F32)]
    for turn in range(S):
        for r in range(2):
            k = S - 1 - turn if r == 0 else turn
            lanes = slice(r * R, (r + 1) * R)
            up = egot[k, :, (2 + r) * R : (3 + r) * R]
            if turn > 0:
                up = up + acc[r][:, k * R : (k + 1) * R]
            delta = (up * slope[k, :, lanes]).astype(BF16)
            ans[k, :, lanes] = delta
            if turn < S - 1:
                inner = jnp.sum(delta.astype(F32) * pre[k, :, lanes], axis=-1, keepdims=True) * (1.0 / D)
                first = k * R + r * H
                sc = lgot[k, :, first : first + 1].astype(F32)
                sc = sc + lgot[k, :, first + R // 4 : first + R // 4 + 1].astype(F32)
                acc[r] = acc[r] + sc * dot(delta, cgot[k]) - inner * lgot[k].astype(F32)
    for i in range(1, S):
        j = peer(i)
        go(remote(ans.at[j], back.at[me], a_send.at[i], a_recv.at[me], on_section(j)))
    back[me] = ans[me]
    for i in range(1, S):
        j = peer(S - i)
        rows = pl.ds(pl.multiple_of(jnp.where(j < me, j, S - 1 - j) * R, R), R)
        lanes = pl.ds(pl.multiple_of(jnp.where(j < me, 0, T), T), T)
        remote(act_t.at[0], low.at[rows, lanes], t_send.at[i], t_recv.at[j], on_section(j)).wait_recv()
    lower = low[...].astype(F32)
    for i in range(1, S):
        j = peer(S - i)
        remote(ans.at[j], back.at[j], a_send.at[i], a_recv.at[j], on_section(j)).wait_recv()

    answer = back[...].reshape(T, 128)
    deltas = [answer[:, r * R : (r + 1) * R] for r in range(2)]
    turned = answer[:, 0 : 2 * R].astype(F32).T.astype(BF16)
    for r in range(2):
        tokens = slice(r * T, (r + 1) * T)
        seen = lower[:, tokens]
        tall = turned[r * R : (r + 1) * R].astype(F32) * pre_t[r * R : (r + 1) * R]
        sc = scale_t[0:1, tokens]
        pull = jnp.sum(tall, axis=0, keepdims=True) * (-1.0 / D) * (sc * sc)
        mix[:, tokens] = (seen * pull).astype(BF16)
        scaled = (deltas[r].astype(F32) * scale_v[tokens, 0:1]).astype(BF16)
        mix[:, 2 * T + r * R : 2 * T + (r + 1) * R] = dot(low[:, tokens], scaled).astype(BF16)
    W = min(512, CH)

    def terms(q):
        def part(i, carry):
            cols = pl.ds(pl.multiple_of(q * CH + i * W, W), W)
            below = dot(mix[...], lhs[:, cols]).astype(BF16)
            for j in range(S):
                for h in range(2):
                    es[h, j // 2, j % 2, :, cols] = below[j * R + h * H : j * R + (h + 1) * H]
            return carry

        lax.fori_loop(0, CH // W, part, 0)
        go(remote(
            es.at[1 - core, :, :, :, chunk(q)], pe.at[:, :, :, chunk(q)],
            c_send.at[q], c_recv.at[q], on_dp(mate),
        ))

    def down_terms(q):
        def part(i, carry):
            cols = pl.ds(pl.multiple_of(i * W, W), W)
            for r in range(2):
                rows = slice(r * T, (r + 1) * T)
                term = dot(turned[r * R : (r + 1) * R], hv[rows, cols]).astype(BF16)
                for h in range(2):
                    ds[h, r, :, cols] = term[h * H : (h + 1) * H]
            return carry

        lax.fori_loop(0, D // W, part, 0)
        go(remote(ds.at[1 - core], dr, d_send.at[0], d_recv.at[0], on_dp(mate)))

    def down_send(q):
        remote(dr, dr, d_send.at[0], d_recv.at[0], on_dp(mate)).wait_recv()
        dr[...] = (ds[core].astype(F32) + dr[...].astype(F32)).astype(BF16)
        go(remote(dr.at[1], fr, f_send.at[0], f_recv.at[0], on_section(mirror)))

    def step_y(q):
        landed = pe.at[:, :, :, chunk(q)]
        remote(landed, landed, c_send.at[q], c_recv.at[q], on_dp(mate)).wait_recv()
        ss[:, :, :, chunk(q)] = (
            es[core, :, :, :, chunk(q)].astype(F32) + pe[:, :, :, chunk(q)].astype(F32)
        ).astype(BF16)
        for way in range(2):
            go(remote(
                ss.at[:, 1 - yl, :, side(q, way)], yb.at[:, :, side(q, way)],
                ty_send.at[way, q], ty_recv.at[way, q], y_next(way),
            ))

    def step_x(q):
        for way in range(2):
            landed = yb.at[:, :, side(q, way)]
            remote(landed, landed, ty_send.at[way, q], ty_recv.at[way, q], y_next(way)).wait_recv()
        xs[:, :, chunk(q)] = (
            ss[:, yl, :, chunk(q)].astype(F32) + yb[:, :, chunk(q)].astype(F32)
        ).astype(BF16)
        for i in range(1, X):
            k = x_peer(i)
            go(remote(xs.at[k, :, chunk(q)], xr.at[x, :, chunk(q)], tx_send.at[i, q], tx_recv.at[x, q], in_row(k)))

    def step_z(q):
        for i in range(1, X):
            k = x_peer(X - i)
            landed = xr.at[k, :, chunk(q)]
            remote(landed, landed, tx_send.at[i, q], tx_recv.at[k, q], in_row(k)).wait_recv()
        if q == 0:
            remote(fr, fr, f_send.at[0], f_recv.at[0], on_section(mirror)).wait_recv()
            remote(own_r, own_r, o_send.at[0], o_recv.at[0], on_dp(mate)).wait_recv()
        whole = own_s[core, :, chunk(q)] + own_r[:, chunk(q)] + xs[x, :, chunk(q)].astype(F32)
        for k in range(X):
            whole = whole + xr[k, :, chunk(q)].astype(F32)
        zs[0:H, chunk(q)] = whole.astype(BF16)
        zs[H:R, chunk(q)] = (dr[0, :, chunk(q)].astype(F32) + fr[:, chunk(q)].astype(F32)).astype(BF16)
        for i in range(1, NZ):
            k = lax.rem(z + i, NZ)
            source = pl.ds(pl.multiple_of(q * CH + k * 128, 128), 128)
            go(remote(
                zs.at[:, source], zr.at[z, :, pl.ds(q * 128, 128)],
                z_send.at[i, q], z_recv.at[z, q], on_dp(place(yh, k)),
            ))
        zr[z, :, q * 128 : (q + 1) * 128] = zs[:, pl.ds(pl.multiple_of(q * CH + z * 128, 128), 128)]

    def y_copy(q, c):
        return remote(
            zt.at[q], yr.at[core, yh], y_send.at[c, q], y_recv.at[core, yh], on_dp(place(q, z, c))
        )

    def on_other(q, c, act):
        @pl.when((yh != q) | (core != c))
        def _():
            act()

    def step_yh(q):
        for i in range(1, NZ):
            k = lax.rem(z + NZ - i, NZ)
            landed = zr.at[k, :, pl.ds(q * 128, 128)]
            remote(landed, landed, z_send.at[i, q], z_recv.at[k, q], on_dp(place(yh, k))).wait_recv()
        whole = zr[0, :, q * 128 : (q + 1) * 128].astype(F32)
        for k in range(1, NZ):
            whole = whole + zr[k, :, q * 128 : (q + 1) * 128].astype(F32)
        zt[q] = whole

        for c in range(CORES):
            on_other(q, c, lambda: y_copy(q, c).start())

        @pl.when(yh == q)
        def _():
            yr[core, q] = zt[q]

    steps = [(terms, 0.0), (step_y, 1.1), (step_x, 3.9), (step_z, 6.9), (step_yh, 9.9)]
    order = [(q + late_by, step, q) for step, late_by in steps for q in range(NY)]
    order += [(0.5, down_terms, 0), (1.15, down_send, 0)]
    for _, step, q in sorted(order, key=lambda entry: entry[0]):
        step(q)

    for c in range(CORES):
        for k in range(NY):
            landed = yr.at[c, k]
            copy = remote(landed, landed, y_send.at[c, k], y_recv.at[c, k], on_dp(place(k, z, c)))
            on_other(k, c, copy.wait_recv)
    for c in range(CORES):
        whole = yr[c, 0]
        for k in range(1, NY):
            whole = whole + yr[c, k]
        out[c] = whole

    for copy in sent:
        copy.wait_send()
    for q in range(NY):
        for c in range(CORES):
            on_other(q, c, y_copy(q, c).wait_send)


def own_columns(parts, out_in, out_out):
    core = lax.rem(lax.axis_index("dp"), CORES)
    H = parts.shape[1] // 2
    for h in range(2):
        chosen = jnp.where(core == 0, parts[h, :, :64], parts[h, :, 64:])
        out_out[h * H : (h + 1) * H, :] = chosen[:H]
        out_in[h * H : (h + 1) * H, :] = chosen[H:]


def on_device(rings, saved, top_grad, gains, adapter_in, adapter_out):
    S = lax.axis_size("section")
    NY, NZ = rings
    _, _, T, D = saved.shape
    R = adapter_in.shape[3]
    X, NL, H, Q = S // 2, S * R, R // 2, T // S
    dma = pltpu.SemaphoreType.DMA
    scratch = [
        pltpu.VMEM((2 * T + 2 * R, D), BF16),
        pltpu.VMEM((2 * T, D), BF16),
        pltpu.VMEM((2 * T, D), BF16),
        pltpu.VMEM((2, D), F32),
        pltpu.VMEM((2, R, D), BF16),
        pltpu.VMEM((2, R, D), BF16),
        pltpu.VMEM((X, 2, R, D), BF16),
        pltpu.VMEM((2 * T, 128), F32),
        pltpu.VMEM((8, 2 * T), F32),
        pltpu.VMEM((T, 2 * R), F32),
        pltpu.VMEM((2 * R, T), F32),
        pltpu.VMEM((NL, 2 * T + 2 * R), BF16),
        pltpu.VMEM((T, 4 * R), F32),
        pltpu.VMEM((T, NL), BF16),
        pltpu.VMEM((R, NL), BF16),
        pltpu.VMEM((S, Q, 4 * R), F32),
        pltpu.VMEM((S, Q, NL), BF16),
        pltpu.VMEM((S, R, NL), BF16),
        pltpu.VMEM((2, R, T), BF16),
        pltpu.VMEM((NL, 2 * T), BF16),
        pltpu.VMEM((R, 2 * T), BF16),
        pltpu.VMEM((S, Q, 128), BF16),
        pltpu.VMEM((S, Q, 128), BF16),
        pltpu.VMEM((2, H, D), F32),
        pltpu.VMEM((H, D), F32),
        pltpu.VMEM((2, 2, H, D), BF16),
        pltpu.VMEM((2, H, D), BF16),
        pltpu.VMEM((2, X, 2, H, D), BF16),
        pltpu.VMEM((X, 2, H, D), BF16),
        pltpu.VMEM((X, 2, H, D), BF16),
        pltpu.VMEM((X, H, D), BF16),
        pltpu.VMEM((X, H, D), BF16),
        pltpu.VMEM((X, H, D), BF16),
        pltpu.VMEM((H, D), BF16),
        pltpu.VMEM((R, D), BF16),
        pltpu.VMEM((NZ, R, NY * 128), BF16),
        pltpu.VMEM((NY, R, 128), F32),
        pltpu.VMEM((CORES, NY, R, 128), F32),
        dma((9,)),
    ]
    scratch += [dma((X,))] * 2 + [dma((S,))] * 2 + [dma((2,))] * 4 + [dma((4,))] * 2
    scratch += [dma((S,))] * 4 + [dma((1,))] * 2 + [dma((S,))] * 4
    scratch += [dma((S,))] * 2 + [dma((1,))] * 4 + [dma((NY,))] * 2 + [dma((2, NY))] * 2
    scratch += [dma((X, NY))] * 2 + [dma((1,))] * 2
    scratch += [dma((NZ, NY))] * 2 + [dma((CORES, NY))] * 2
    half = D // (NY * NZ * CORES)
    vmem = pl.BlockSpec(memory_space=pltpu.VMEM)
    parts = pl.pallas_call(
        partial(kernel, (S, NY, NZ, T, D, R)),
        out_shape=jax.ShapeDtypeStruct((2, R, 128), F32),
        in_specs=[pl.BlockSpec(memory_space=pl.ANY)] * 5,
        out_specs=vmem,
        scratch_shapes=scratch,
        compiler_params=pltpu.CompilerParams(
            collective_id=0, has_side_effects=True, vmem_limit_bytes=56 * 2**20
        ),
        cost_estimate=pl.CostEstimate(
            flops=4 * 10**9, bytes_accessed=6 * 2**20, transcendentals=2 * T * R
        ),
    )(saved, top_grad, gains, jnp.swapaxes(adapter_in, 2, 3), adapter_out)
    shape = jax.ShapeDtypeStruct((R, half), F32)
    grad_in, grad_out = pl.pallas_call(
        own_columns, out_shape=(shape, shape), in_specs=[vmem], out_specs=(vmem, vmem)
    )(parts)
    return (grad_in.T[None], grad_out[None])


def solution(mesh):
    in_specs = (
        P("section", None, "dp", None),
        P(None, "dp", None),
        P("section", None, None),
        P("section", None, None, None),
        P("section", None, None, None),
    )
    out_specs = (P("section", "dp", None), P("section", None, "dp"))
    return jax.shard_map(
        partial(on_device, RINGS[mesh.shape["dp"]]),
        mesh=mesh, in_specs=in_specs, out_specs=out_specs, check_vma=False,
    )
```

```python
from functools import partial

import jax
import jax.numpy as jnp
from jax import lax
from jax.experimental import pallas as pl
from jax.experimental.pallas import tpu as pltpu
from jax.sharding import PartitionSpec as P

EPS = 1e-05
CORES = 2
RINGS = {64: (4, 8), 8: (2, 2), 4: (1, 2)}
BF16 = jnp.bfloat16
F32 = jnp.float32


def over_last(a, b):
    return lax.dot_general(a, b, (((1,), (1,)), ((), ())), preferred_element_type=F32)


def dot(a, b):
    return jnp.dot(a, b, preferred_element_type=F32)


def kernel(
    dims, saved, top, gains, win, wout, out,
    lhs, tv, hv, gv, iv, ov, wall, scale_v, scale_t, pre_v, pre_t, mix, early, late, coup, egot, lgot, cgot,
    act_t, low, same, ans, back, own_s, own_r, ds, dr, es, pe, ss, yb, xs, xr, fr, zs, zr, zt, yr,
    load_sem, wx_send, wx_recv, wd_send, wd_recv, wy_send, wy_recv, wz_send, wz_recv, wc_send, wc_recv,
    e_send, e_recv, t_send, t_recv, g_send, g_recv, v_send, v_recv, k_send, k_recv,
    a_send, a_recv, o_send, o_recv, d_send, d_recv, c_send, c_recv, ty_send, ty_recv, tx_send, tx_recv, f_send, f_recv,
    z_send, z_recv, y_send, y_recv,
):
    S, NY, NZ, T, D, R = dims
    X = S // 2
    NL = S * R
    H = R // 2
    Q = T // S
    CH = D // NY
    me = lax.axis_index("section")
    dp = lax.axis_index("dp")
    x = me // 2
    yl = lax.rem(me, 2)
    core = lax.rem(dp, CORES)
    z = lax.rem(dp // CORES, NZ)
    yh = dp // (CORES * NZ)
    mate = dp + 1 - 2 * core
    mirror = S - 1 - me
    far = lax.rem(yh + 2 * yl + NY - 1, NY)
    NEAR = 128 * (3 * CH // 1024) if CH >= 1024 else CH // 2
    beside = 2 * x + 1 - yl

    def on_section(j):
        return {"section": j, "dp": dp}

    def on_dp(k):
        return {"section": me, "dp": k}

    def place(h, k, c=None):
        return h * (NZ * CORES) + k * CORES + (core if c is None else c)

    def y_next(way):
        return {"section": beside, "dp": dp if way == 0 else place(far, z)}

    def side(q, way):
        return pl.ds(q * CH, NEAR) if way == 0 else pl.ds(q * CH + NEAR, CH - NEAR)

    def peer(i):
        return lax.rem(me + i, S)

    def x_peer(i):
        return lax.rem(x + i, X)

    def in_row(k):
        return on_section(2 * k + yl)

    def remote(src, dst, send, recv, device):
        return pltpu.make_async_remote_copy(
            src_ref=src, dst_ref=dst, send_sem=send, recv_sem=recv,
            device_id=device, device_id_type=pl.DeviceIdType.MESH,
        )

    sent = []

    def go(copy):
        copy.start()
        sent.append(copy)

    def chunk(q):
        return pl.ds(q * CH, CH)

    half = pl.ds(pl.multiple_of(core * H, H), H)
    other_half = pl.ds(pl.multiple_of((1 - core) * H, H), H)
    steps_of = [(0, 1)] + [(dx, dy) for dx in sorted(range(1, X), key=lambda n: min(n, X - n)) for dy in range(2)]

    def section_at(dx, dy, sign=1):
        return 2 * lax.rem(x + X + sign * dx, X) + (1 - yl if dy else yl)

    barrier = pltpu.get_barrier_semaphore()
    greeted = [on_section(peer(i)) for i in range(1, S)] + [on_dp(mate)]
    greeted += [{"section": beside, "dp": place(far, z)}]
    greeted += [on_dp(place(yh, lax.rem(z + i, NZ))) for i in range(1, NZ)]
    greeted += [on_dp(place(lax.rem(yh + i, NY), z, c)) for i in range(1, NY) for c in range(CORES)]
    for device in greeted:
        pl.semaphore_signal(barrier, inc=1, device_id=device, device_id_type=pl.DeviceIdType.MESH)

    near = pl.ds(0, D // 2)
    E = D // 4
    odd = lax.rem(z, 2)
    mine_z = pl.ds(pl.multiple_of(D // 2 + odd * E, E), E)
    theirs_z = pl.ds(pl.multiple_of(D // 2 + (1 - odd) * E, E), E)
    own_units = [
        pltpu.make_async_copy(wout.at[0, yl, half, cols], wall.at[x, yl, half, cols], load_sem.at[7 + n])
        for n, cols in enumerate((near, mine_z))
    ]
    for copy in own_units:
        copy.start()

    loads = []
    for r in range(2):
        rows = pl.ds(r * T, T)
        loads.append(pltpu.make_async_copy(saved.at[0, r], lhs.at[rows], load_sem.at[r]))
    loads.append(pltpu.make_async_copy(gains.at[0], gv, load_sem.at[2]))
    loads.append(pltpu.make_async_copy(win.at[0], iv, load_sem.at[3]))
    loads.append(pltpu.make_async_copy(wout.at[0], ov, load_sem.at[4]))
    for r in range(2):
        rows = pl.ds(r * T, T)
        loads.append(pltpu.make_async_copy(top.at[r], tv.at[rows], load_sem.at[5 + r]))
    for copy in loads:
        copy.start()

    pl.semaphore_wait(barrier, len(greeted))

    def upper(j):
        return jnp.where(j > me, 0, 1)

    for i in range(1, X):
        j = 2 * x_peer(i) + yl
        go(remote(
            wout.at[0, upper(j), half, near], wall.at[x, yl, half, near], wx_send.at[i], wx_recv.at[x], on_section(j)
        ))
    for n, (dx, dy) in reversed(list(enumerate(steps_of))):
        j = section_at(dx, dy)
        go(remote(
            wout.at[0, upper(j), half, mine_z], wall.at[x, yl, half, mine_z],
            wd_send.at[n], wd_recv.at[me], on_section(j),
        ))

    for j in range(S):
        @pl.when(j >= me)
        def _():
            low[j * R : (j + 1) * R, 0:T] = jnp.zeros((R, T), BF16)

        @pl.when(j >= mirror)
        def _():
            low[j * R : (j + 1) * R, T : 2 * T] = jnp.zeros((R, T), BF16)

    xr[x] = jnp.zeros((H, D), BF16)

    def onward(way):
        return pl.ds(way * E, E)

    def onward_z(way, parity):
        return pl.ds(pl.multiple_of(D // 2 + parity * E + way * (E // 2), E // 2), E // 2)

    def z_next(way):
        return on_dp(place(yh, lax.rem(z + (1 if way == 0 else NZ - 1), NZ)))

    def gather_row():
        own_units[0].wait()
        for i in range(1, X):
            k = x_peer(X - i)
            landed = wall.at[k, yl, half, near]
            remote(landed, landed, wx_send.at[i], wx_recv.at[k], in_row(k)).wait_recv()
        for way in range(2):
            row = wall.at[:, yl, half, onward(way)]
            go(remote(row, row, wy_send.at[way], wy_recv.at[way], y_next(way)))
        row = wall.at[:, yl, half, near]
        go(remote(row, row, wc_send.at[0], wc_recv.at[0], on_dp(mate)))

    def gather_direct():
        own_units[1].wait()
        for n, (dx, dy) in enumerate(steps_of):
            j = section_at(dx, dy, -1)
            landed = wall.at[j // 2, lax.rem(j, 2), half, mine_z]
            remote(landed, landed, wd_send.at[n], wd_recv.at[j], on_section(j)).wait_recv()
        for way in range(2):
            part = wall.at[:, :, half, onward_z(way, odd)]
            go(remote(part, part, wz_send.at[way], wz_recv.at[way], z_next(way)))
        part = wall.at[:, :, half, mine_z]
        go(remote(part, part, wc_send.at[1], wc_recv.at[1], on_dp(mate)))

    def gather_y():
        for way in range(2):
            row = wall.at[:, 1 - yl, half, onward(way)]
            remote(row, row, wy_send.at[way], wy_recv.at[way], y_next(way)).wait_recv()
        row = wall.at[:, 1 - yl, half, near]
        go(remote(row, row, wc_send.at[2], wc_recv.at[2], on_dp(mate)))

    def gather_z():
        for way in range(2):
            part = wall.at[:, :, half, onward_z(way, 1 - odd)]
            remote(part, part, wz_send.at[way], wz_recv.at[way], z_next(way)).wait_recv()
        part = wall.at[:, :, half, theirs_z]
        go(remote(part, part, wc_send.at[3], wc_recv.at[3], on_dp(mate)))

    def project_near():
        for n, line in ((0, yl), (2, 1 - yl)):
            row = wall.at[:, line, other_half, near]
            remote(row, row, wc_send.at[n], wc_recv.at[n], on_dp(mate)).wait_recv()
        return over_last(lhs[:, : D // 2], wall[:, :, :, : D // 2].reshape(NL, D // 2))

    def project_rest(n, cols):
        part = wall.at[:, :, other_half, cols]
        remote(part, part, wc_send.at[n], wc_recv.at[n], on_dp(mate)).wait_recv()
        return over_last(lhs[:, cols], wall[:, :, :, cols].reshape(NL, E))

    def piece_norm():
        for n in range(2):
            loads[n].wait()

        def squares(i, acc):
            xf = lhs[0 : 2 * T, pl.ds(pl.multiple_of(i * 128, 128), 128)].astype(F32)
            return acc + xf * xf

        total = lax.fori_loop(0, D // 128, squares, jnp.zeros((2 * T, 128), F32), unroll=2)
        scale = lax.rsqrt(jnp.sum(total, axis=-1, keepdims=True) * (1.0 / D) + EPS)
        wide = jnp.broadcast_to(scale, (2 * T, 128))
        scale_v[...] = wide
        scale_t[...] = wide.T[0:8]

    def piece_hidden():
        for n in range(2, 5):
            loads[n].wait()

        def normed(i, carry):
            cols = pl.ds(pl.multiple_of(i * 128, 128), 128)
            for r in range(2):
                rows = slice(r * T, (r + 1) * T)
                nf = lhs[rows, cols].astype(F32) * scale_v[rows, :]
                hv[rows, cols] = (nf * gv[r : r + 1, cols]).astype(BF16)
                lhs[2 * T + r * R : 2 * T + (r + 1) * R, cols] = (
                    iv[r, :, cols].astype(F32) * gv[r : r + 1, cols]
                ).astype(BF16)
            return carry

        lax.fori_loop(0, D // 128, normed, 0)

    def piece_down():
        for r in range(2):
            rows = slice(r * T, (r + 1) * T)
            pre = over_last(hv[rows, :], iv[r])
            pre_v[:, r * R : (r + 1) * R] = pre
            early[:, r * R : (r + 1) * R] = pre
        pre = pre_v[...].T
        pre_t[...] = pre
        active = pre * jax.nn.sigmoid(pre)
        for r in range(2):
            act_t[r] = active[r * R : (r + 1) * R].astype(BF16)
        same[:, 0:T] = act_t[0]
        for i in range(1, S):
            j = peer(i)
            replica = jnp.where(j > me, 0, 1)
            rows = pl.ds(pl.multiple_of(jnp.where(j > me, me, mirror) * R, R), R)
            lanes = pl.ds(pl.multiple_of(replica * T, T), T)
            go(remote(act_t.at[replica], low.at[rows, lanes], t_send.at[i], t_recv.at[me], on_section(j)))
        go(remote(act_t.at[1], same.at[:, pl.ds(T, T)], g_send.at[0], g_recv.at[0], on_section(mirror)))

    def piece_up():
        for n in range(5, 7):
            loads[n].wait()
        for r in range(2):
            rows = slice(r * T, (r + 1) * T)
            early[:, (2 + r) * R : (3 + r) * R] = over_last(tv[rows, :], ov[r])
        for i in range(1, S):
            j = peer(i)
            rows = pl.ds(pl.multiple_of(j * Q, Q), Q)
            go(remote(early.at[rows], egot.at[me], e_send.at[i], e_recv.at[me], on_section(j)))
        egot[me] = early[pl.ds(pl.multiple_of(me * Q, Q), Q), :]

    piece_norm()
    piece_hidden()
    gather_row()
    gather_direct()
    piece_down()
    piece_up()
    across = project_rest(1, mine_z)
    gather_y()
    gather_z()
    across = across + project_near()
    across = across + project_rest(3, theirs_z)

    block = lax.broadcasted_iota(jnp.int32, (R, NL), 1) // R
    coup[...] = jnp.where(
        block < me, across[2 * T : 2 * T + R], across[2 * T + R :]
    ).astype(BF16)
    lane = lax.broadcasted_iota(jnp.int32, (T, NL), 1)
    block = lane // R
    within = lax.rem(lane, R) // (R // 4)
    sc0 = scale_v[:T, 0:1]
    sc1 = scale_v[T:, 0:1]
    sc = jnp.where(within < 2, sc0, sc1)
    rounded = sc.astype(BF16).astype(F32)
    own = jnp.where(lax.rem(within, 2) == 0, rounded, sc - rounded)
    late[...] = jnp.where(
        block < me, across[:T] * (sc0 * sc0), jnp.where(block > me, across[T : 2 * T] * (sc1 * sc1), own)
    ).astype(BF16)
    for i in range(1, S):
        j = peer(i)
        rows = pl.ds(pl.multiple_of(j * Q, Q), Q)
        go(remote(coup, cgot.at[me], k_send.at[i], k_recv.at[me], on_section(j)))
        go(remote(late.at[rows], lgot.at[me], v_send.at[i], v_recv.at[me], on_section(j)))
    cgot[me] = coup[...]
    lgot[me] = late[pl.ds(pl.multiple_of(me * Q, Q), Q), :]

    remote(act_t.at[1], same.at[:, pl.ds(T, T)], g_send.at[0], g_recv.at[0], on_section(mirror)).wait_recv()
    for q in range(NY):
        term = dot(same[...], tv[:, chunk(q)])
        for h in range(2):
            own_s[h, :, chunk(q)] = term[h * H : (h + 1) * H]
    go(remote(own_s.at[1 - core], own_r, o_send.at[0], o_recv.at[0], on_dp(mate)))

    for i in range(1, S):
        j = peer(S - i)
        remote(early.at[pl.ds(0, Q)], egot.at[j], e_send.at[i], e_recv.at[j], on_section(j)).wait_recv()
    pre = egot[:, :, 0 : 2 * R]
    sig = jax.nn.sigmoid(pre)
    slope = sig * (1.0 + pre * (1.0 - sig))
    for i in range(1, S):
        j = peer(S - i)
        remote(coup, cgot.at[j], k_send.at[i], k_recv.at[j], on_section(j)).wait_recv()
        remote(late.at[pl.ds(0, Q)], lgot.at[j], v_send.at[i], v_recv.at[j], on_section(j)).wait_recv()

    acc = [jnp.zeros((Q, NL), F32), jnp.zeros((Q, NL), F32)]
    for turn in range(S):
        for r in range(2):
            k = S - 1 - turn if r == 0 else turn
            lanes = slice(r * R, (r + 1) * R)
            up = egot[k, :, (2 + r) * R : (3 + r) * R]
            if turn > 0:
                up = up + acc[r][:, k * R : (k + 1) * R]
            delta = (up * slope[k, :, lanes]).astype(BF16)
            ans[k, :, lanes] = delta
            if turn < S - 1:
                inner = jnp.sum(delta.astype(F32) * pre[k, :, lanes], axis=-1, keepdims=True) * (1.0 / D)
                first = k * R + r * H
                sc = lgot[k, :, first : first + 1].astype(F32)
                sc = sc + lgot[k, :, first + R // 4 : first + R // 4 + 1].astype(F32)
                acc[r] = acc[r] + sc * dot(delta, cgot[k]) - inner * lgot[k].astype(F32)
    for i in range(1, S):
        j = peer(i)
        go(remote(ans.at[j], back.at[me], a_send.at[i], a_recv.at[me], on_section(j)))
    back[me] = ans[me]
    for i in range(1, S):
        j = peer(S - i)
        rows = pl.ds(pl.multiple_of(jnp.where(j < me, j, S - 1 - j) * R, R), R)
        lanes = pl.ds(pl.multiple_of(jnp.where(j < me, 0, T), T), T)
        remote(act_t.at[0], low.at[rows, lanes], t_send.at[i], t_recv.at[j], on_section(j)).wait_recv()
    lower = low[...].astype(F32)
    for i in range(1, S):
        j = peer(S - i)
        remote(ans.at[j], back.at[j], a_send.at[i], a_recv.at[j], on_section(j)).wait_recv()

    answer = back[...].reshape(T, 128)
    deltas = [answer[:, r * R : (r + 1) * R] for r in range(2)]
    turned = answer[:, 0 : 2 * R].astype(F32).T.astype(BF16)
    for r in range(2):
        tokens = slice(r * T, (r + 1) * T)
        seen = lower[:, tokens]
        tall = turned[r * R : (r + 1) * R].astype(F32) * pre_t[r * R : (r + 1) * R]
        sc = scale_t[0:1, tokens]
        pull = jnp.sum(tall, axis=0, keepdims=True) * (-1.0 / D) * (sc * sc)
        mix[:, tokens] = (seen * pull).astype(BF16)
        scaled = (deltas[r].astype(F32) * scale_v[tokens, 0:1]).astype(BF16)
        mix[:, 2 * T + r * R : 2 * T + (r + 1) * R] = dot(low[:, tokens], scaled).astype(BF16)
    W = min(512, CH)

    def terms(q):
        def part(i, carry):
            cols = pl.ds(pl.multiple_of(q * CH + i * W, W), W)
            below = dot(mix[...], lhs[:, cols]).astype(BF16)
            for j in range(S):
                for h in range(2):
                    es[h, j // 2, j % 2, :, cols] = below[j * R + h * H : j * R + (h + 1) * H]
            return carry

        lax.fori_loop(0, CH // W, part, 0)
        go(remote(
            es.at[1 - core, :, :, :, chunk(q)], pe.at[:, :, :, chunk(q)],
            c_send.at[q], c_recv.at[q], on_dp(mate),
        ))

    def down_terms(q):
        def part(i, carry):
            cols = pl.ds(pl.multiple_of(i * W, W), W)
            for r in range(2):
                rows = slice(r * T, (r + 1) * T)
                term = dot(turned[r * R : (r + 1) * R], hv[rows, cols]).astype(BF16)
                for h in range(2):
                    ds[h, r, :, cols] = term[h * H : (h + 1) * H]
            return carry

        lax.fori_loop(0, D // W, part, 0)
        go(remote(ds.at[1 - core], dr, d_send.at[0], d_recv.at[0], on_dp(mate)))

    def down_send(q):
        remote(dr, dr, d_send.at[0], d_recv.at[0], on_dp(mate)).wait_recv()
        dr[...] = (ds[core].astype(F32) + dr[...].astype(F32)).astype(BF16)
        go(remote(dr.at[1], fr, f_send.at[0], f_recv.at[0], on_section(mirror)))

    def step_y(q):
        landed = pe.at[:, :, :, chunk(q)]
        remote(landed, landed, c_send.at[q], c_recv.at[q], on_dp(mate)).wait_recv()
        ss[:, :, :, chunk(q)] = (
            es[core, :, :, :, chunk(q)].astype(F32) + pe[:, :, :, chunk(q)].astype(F32)
        ).astype(BF16)
        for way in range(2):
            go(remote(
                ss.at[:, 1 - yl, :, side(q, way)], yb.at[:, :, side(q, way)],
                ty_send.at[way, q], ty_recv.at[way, q], y_next(way),
            ))

    def step_x(q):
        for way in range(2):
            landed = yb.at[:, :, side(q, way)]
            remote(landed, landed, ty_send.at[way, q], ty_recv.at[way, q], y_next(way)).wait_recv()
        xs[:, :, chunk(q)] = (
            ss[:, yl, :, chunk(q)].astype(F32) + yb[:, :, chunk(q)].astype(F32)
        ).astype(BF16)
        for i in range(1, X):
            k = x_peer(i)
            go(remote(xs.at[k, :, chunk(q)], xr.at[x, :, chunk(q)], tx_send.at[i, q], tx_recv.at[x, q], in_row(k)))

    def step_z(q):
        for i in range(1, X):
            k = x_peer(X - i)
            landed = xr.at[k, :, chunk(q)]
            remote(landed, landed, tx_send.at[i, q], tx_recv.at[k, q], in_row(k)).wait_recv()
        if q == 0:
            remote(fr, fr, f_send.at[0], f_recv.at[0], on_section(mirror)).wait_recv()
            remote(own_r, own_r, o_send.at[0], o_recv.at[0], on_dp(mate)).wait_recv()
        whole = own_s[core, :, chunk(q)] + own_r[:, chunk(q)] + xs[x, :, chunk(q)].astype(F32)
        for k in range(X):
            whole = whole + xr[k, :, chunk(q)].astype(F32)
        zs[0:H, chunk(q)] = whole.astype(BF16)
        zs[H:R, chunk(q)] = (dr[0, :, chunk(q)].astype(F32) + fr[:, chunk(q)].astype(F32)).astype(BF16)
        for i in range(1, NZ):
            k = lax.rem(z + i, NZ)
            source = pl.ds(pl.multiple_of(q * CH + k * 128, 128), 128)
            go(remote(
                zs.at[:, source], zr.at[z, :, pl.ds(q * 128, 128)],
                z_send.at[i, q], z_recv.at[z, q], on_dp(place(yh, k)),
            ))
        zr[z, :, q * 128 : (q + 1) * 128] = zs[:, pl.ds(pl.multiple_of(q * CH + z * 128, 128), 128)]

    def y_copy(q, c):
        return remote(
            zt.at[q], yr.at[core, yh], y_send.at[c, q], y_recv.at[core, yh], on_dp(place(q, z, c))
        )

    def on_other(q, c, act):
        @pl.when((yh != q) | (core != c))
        def _():
            act()

    def step_yh(q):
        for i in range(1, NZ):
            k = lax.rem(z + NZ - i, NZ)
            landed = zr.at[k, :, pl.ds(q * 128, 128)]
            remote(landed, landed, z_send.at[i, q], z_recv.at[k, q], on_dp(place(yh, k))).wait_recv()
        whole = zr[0, :, q * 128 : (q + 1) * 128].astype(F32)
        for k in range(1, NZ):
            whole = whole + zr[k, :, q * 128 : (q + 1) * 128].astype(F32)
        zt[q] = whole

        for c in range(CORES):
            on_other(q, c, lambda: y_copy(q, c).start())

        @pl.when(yh == q)
        def _():
            yr[core, q] = zt[q]

    steps = [(terms, 0.0), (step_y, 1.1), (step_x, 3.9), (step_z, 6.4), (step_yh, 9.4)]
    order = [(q + late_by, step, q) for step, late_by in steps for q in range(NY)]
    order += [(0.5, down_terms, 0), (1.15, down_send, 0)]
    for _, step, q in sorted(order, key=lambda entry: entry[0]):
        step(q)

    for c in range(CORES):
        for k in range(NY):
            landed = yr.at[c, k]
            copy = remote(landed, landed, y_send.at[c, k], y_recv.at[c, k], on_dp(place(k, z, c)))
            on_other(k, c, copy.wait_recv)
    for c in range(CORES):
        whole = yr[c, 0]
        for k in range(1, NY):
            whole = whole + yr[c, k]
        out[c] = whole

    for copy in sent:
        copy.wait_send()
    for q in range(NY):
        for c in range(CORES):
            on_other(q, c, y_copy(q, c).wait_send)


def own_columns(parts, out_in, out_out):
    core = lax.rem(lax.axis_index("dp"), CORES)
    H = parts.shape[1] // 2
    for h in range(2):
        chosen = jnp.where(core == 0, parts[h, :, :64], parts[h, :, 64:])
        out_out[h * H : (h + 1) * H, :] = chosen[:H]
        out_in[h * H : (h + 1) * H, :] = chosen[H:]


def on_device(rings, saved, top_grad, gains, adapter_in, adapter_out):
    S = lax.axis_size("section")
    NY, NZ = rings
    _, _, T, D = saved.shape
    R = adapter_in.shape[3]
    X, NL, H, Q = S // 2, S * R, R // 2, T // S
    dma = pltpu.SemaphoreType.DMA
    scratch = [
        pltpu.VMEM((2 * T + 2 * R, D), BF16),
        pltpu.VMEM((2 * T, D), BF16),
        pltpu.VMEM((2 * T, D), BF16),
        pltpu.VMEM((2, D), F32),
        pltpu.VMEM((2, R, D), BF16),
        pltpu.VMEM((2, R, D), BF16),
        pltpu.VMEM((X, 2, R, D), BF16),
        pltpu.VMEM((2 * T, 128), F32),
        pltpu.VMEM((8, 2 * T), F32),
        pltpu.VMEM((T, 2 * R), F32),
        pltpu.VMEM((2 * R, T), F32),
        pltpu.VMEM((NL, 2 * T + 2 * R), BF16),
        pltpu.VMEM((T, 4 * R), F32),
        pltpu.VMEM((T, NL), BF16),
        pltpu.VMEM((R, NL), BF16),
        pltpu.VMEM((S, Q, 4 * R), F32),
        pltpu.VMEM((S, Q, NL), BF16),
        pltpu.VMEM((S, R, NL), BF16),
        pltpu.VMEM((2, R, T), BF16),
        pltpu.VMEM((NL, 2 * T), BF16),
        pltpu.VMEM((R, 2 * T), BF16),
        pltpu.VMEM((S, Q, 128), BF16),
        pltpu.VMEM((S, Q, 128), BF16),
        pltpu.VMEM((2, H, D), F32),
        pltpu.VMEM((H, D), F32),
        pltpu.VMEM((2, 2, H, D), BF16),
        pltpu.VMEM((2, H, D), BF16),
        pltpu.VMEM((2, X, 2, H, D), BF16),
        pltpu.VMEM((X, 2, H, D), BF16),
        pltpu.VMEM((X, 2, H, D), BF16),
        pltpu.VMEM((X, H, D), BF16),
        pltpu.VMEM((X, H, D), BF16),
        pltpu.VMEM((X, H, D), BF16),
        pltpu.VMEM((H, D), BF16),
        pltpu.VMEM((R, D), BF16),
        pltpu.VMEM((NZ, R, NY * 128), BF16),
        pltpu.VMEM((NY, R, 128), F32),
        pltpu.VMEM((CORES, NY, R, 128), F32),
        dma((9,)),
    ]
    scratch += [dma((X,))] * 2 + [dma((S,))] * 2 + [dma((2,))] * 4 + [dma((4,))] * 2
    scratch += [dma((S,))] * 4 + [dma((1,))] * 2 + [dma((S,))] * 4
    scratch += [dma((S,))] * 2 + [dma((1,))] * 4 + [dma((NY,))] * 2 + [dma((2, NY))] * 2
    scratch += [dma((X, NY))] * 2 + [dma((1,))] * 2
    scratch += [dma((NZ, NY))] * 2 + [dma((CORES, NY))] * 2
    half = D // (NY * NZ * CORES)
    vmem = pl.BlockSpec(memory_space=pltpu.VMEM)
    parts = pl.pallas_call(
        partial(kernel, (S, NY, NZ, T, D, R)),
        out_shape=jax.ShapeDtypeStruct((2, R, 128), F32),
        in_specs=[pl.BlockSpec(memory_space=pl.ANY)] * 5,
        out_specs=vmem,
        scratch_shapes=scratch,
        compiler_params=pltpu.CompilerParams(
            collective_id=0, has_side_effects=True, vmem_limit_bytes=56 * 2**20
        ),
        cost_estimate=pl.CostEstimate(
            flops=4 * 10**9, bytes_accessed=6 * 2**20, transcendentals=2 * T * R
        ),
    )(saved, top_grad, gains, jnp.swapaxes(adapter_in, 2, 3), adapter_out)
    shape = jax.ShapeDtypeStruct((R, half), F32)
    grad_in, grad_out = pl.pallas_call(
        own_columns, out_shape=(shape, shape), in_specs=[vmem], out_specs=(vmem, vmem)
    )(parts)
    return (grad_in.T[None], grad_out[None])


def solution(mesh):
    in_specs = (
        P("section", None, "dp", None),
        P(None, "dp", None),
        P("section", None, None),
        P("section", None, None, None),
        P("section", None, None, None),
    )
    out_specs = (P("section", "dp", None), P("section", None, "dp"))
    return jax.shard_map(
        partial(on_device, RINGS[mesh.shape["dp"]]),
        mesh=mesh, in_specs=in_specs, out_specs=out_specs, check_vma=False,
    )
```

```python
from functools import partial

import jax
import jax.numpy as jnp
from jax import lax
from jax.experimental import pallas as pl
from jax.experimental.pallas import tpu as pltpu
from jax.sharding import PartitionSpec as P

EPS = 1e-05
CORES = 2
RINGS = {64: (4, 8), 8: (2, 2), 4: (1, 2)}
BF16 = jnp.bfloat16
F32 = jnp.float32


def over_last(a, b):
    return lax.dot_general(a, b, (((1,), (1,)), ((), ())), preferred_element_type=F32)


def dot(a, b):
    return jnp.dot(a, b, preferred_element_type=F32)


def kernel(
    dims, saved, top, gains, win, wout, out,
    lhs, tv, hv, gv, iv, ov, wall, scale_v, scale_t, pre_v, pre_t, mix, early, late, coup, egot, lgot, cgot,
    act_t, low, same, ans, back, own_s, own_r, ds, dr, es, pe, ss, yb, xs, xr, fr, zs, zr, zt, yr,
    load_sem, wx_send, wx_recv, wd_send, wd_recv, wy_send, wy_recv, wz_send, wz_recv, wc_send, wc_recv,
    e_send, e_recv, t_send, t_recv, g_send, g_recv, v_send, v_recv, k_send, k_recv,
    a_send, a_recv, o_send, o_recv, d_send, d_recv, c_send, c_recv, ty_send, ty_recv, tx_send, tx_recv, f_send, f_recv,
    z_send, z_recv, y_send, y_recv,
):
    S, NY, NZ, T, D, R = dims
    X = S // 2
    NL = S * R
    H = R // 2
    Q = T // S
    CH = D // NY
    me = lax.axis_index("section")
    dp = lax.axis_index("dp")
    x = me // 2
    yl = lax.rem(me, 2)
    core = lax.rem(dp, CORES)
    z = lax.rem(dp // CORES, NZ)
    yh = dp // (CORES * NZ)
    mate = dp + 1 - 2 * core
    mirror = S - 1 - me
    far = lax.rem(yh + 2 * yl + NY - 1, NY)
    NEAR = 128 * (3 * CH // 1024) if CH >= 1024 else CH // 2
    beside = 2 * x + 1 - yl

    def on_section(j):
        return {"section": j, "dp": dp}

    def on_dp(k):
        return {"section": me, "dp": k}

    def place(h, k, c=None):
        return h * (NZ * CORES) + k * CORES + (core if c is None else c)

    def y_next(way):
        return {"section": beside, "dp": dp if way == 0 else place(far, z)}

    def side(q, way):
        return pl.ds(q * CH, NEAR) if way == 0 else pl.ds(q * CH + NEAR, CH - NEAR)

    def peer(i):
        return lax.rem(me + i, S)

    def x_peer(i):
        return lax.rem(x + i, X)

    def in_row(k):
        return on_section(2 * k + yl)

    def remote(src, dst, send, recv, device):
        return pltpu.make_async_remote_copy(
            src_ref=src, dst_ref=dst, send_sem=send, recv_sem=recv,
            device_id=device, device_id_type=pl.DeviceIdType.MESH,
        )

    sent = []

    def go(copy):
        copy.start()
        sent.append(copy)

    def chunk(q):
        return pl.ds(q * CH, CH)

    half = pl.ds(pl.multiple_of(core * H, H), H)
    other_half = pl.ds(pl.multiple_of((1 - core) * H, H), H)
    steps_of = [(0, 1)] + [(dx, dy) for dx in sorted(range(1, X), key=lambda n: min(n, X - n)) for dy in range(2)]

    def section_at(dx, dy, sign=1):
        return 2 * lax.rem(x + X + sign * dx, X) + (1 - yl if dy else yl)

    barrier = pltpu.get_barrier_semaphore()
    greeted = [on_section(peer(i)) for i in range(1, S)] + [on_dp(mate)]
    greeted += [{"section": beside, "dp": place(far, z)}]
    greeted += [on_dp(place(yh, lax.rem(z + i, NZ))) for i in range(1, NZ)]
    greeted += [on_dp(place(lax.rem(yh + i, NY), z, c)) for i in range(1, NY) for c in range(CORES)]
    for device in reversed(greeted):
        pl.semaphore_signal(barrier, inc=1, device_id=device, device_id_type=pl.DeviceIdType.MESH)

    near = pl.ds(0, D // 2)
    E = D // 4
    odd = lax.rem(z, 2)
    mine_z = pl.ds(pl.multiple_of(D // 2 + odd * E, E), E)
    theirs_z = pl.ds(pl.multiple_of(D // 2 + (1 - odd) * E, E), E)
    own_units = [
        pltpu.make_async_copy(wout.at[0, yl, half, cols], wall.at[x, yl, half, cols], load_sem.at[7 + n])
        for n, cols in enumerate((near, mine_z))
    ]
    for copy in own_units:
        copy.start()

    loads = []
    for r in range(2):
        rows = pl.ds(r * T, T)
        loads.append(pltpu.make_async_copy(saved.at[0, r], lhs.at[rows], load_sem.at[r]))
    loads.append(pltpu.make_async_copy(gains.at[0], gv, load_sem.at[2]))
    loads.append(pltpu.make_async_copy(win.at[0], iv, load_sem.at[3]))
    loads.append(pltpu.make_async_copy(wout.at[0], ov, load_sem.at[4]))
    for r in range(2):
        rows = pl.ds(r * T, T)
        loads.append(pltpu.make_async_copy(top.at[r], tv.at[rows], load_sem.at[5 + r]))
    for copy in loads:
        copy.start()

    pl.semaphore_wait(barrier, len(greeted))

    def upper(j):
        return jnp.where(j > me, 0, 1)

    for i in range(1, X):
        j = 2 * x_peer(i) + yl
        go(remote(
            wout.at[0, upper(j), half, near], wall.at[x, yl, half, near], wx_send.at[i], wx_recv.at[x], on_section(j)
        ))
    for n, (dx, dy) in reversed(list(enumerate(steps_of))):
        j = section_at(dx, dy)
        go(remote(
            wout.at[0, upper(j), half, mine_z], wall.at[x, yl, half, mine_z],
            wd_send.at[n], wd_recv.at[me], on_section(j),
        ))

    for j in range(S):
        @pl.when(j >= me)
        def _():
            low[j * R : (j + 1) * R, 0:T] = jnp.zeros((R, T), BF16)

        @pl.when(j >= mirror)
        def _():
            low[j * R : (j + 1) * R, T : 2 * T] = jnp.zeros((R, T), BF16)

    xr[x] = jnp.zeros((H, D), BF16)

    def onward(way):
        return pl.ds(way * E, E)

    def onward_z(way, parity):
        return pl.ds(pl.multiple_of(D // 2 + parity * E + way * (E // 2), E // 2), E // 2)

    def z_next(way):
        return on_dp(place(yh, lax.rem(z + (1 if way == 0 else NZ - 1), NZ)))

    def gather_row():
        own_units[0].wait()
        for i in range(1, X):
            k = x_peer(X - i)
            landed = wall.at[k, yl, half, near]
            remote(landed, landed, wx_send.at[i], wx_recv.at[k], in_row(k)).wait_recv()
        for way in range(2):
            row = wall.at[:, yl, half, onward(way)]
            go(remote(row, row, wy_send.at[way], wy_recv.at[way], y_next(way)))
        row = wall.at[:, yl, half, near]
        go(remote(row, row, wc_send.at[0], wc_recv.at[0], on_dp(mate)))

    def gather_direct():
        own_units[1].wait()
        for n, (dx, dy) in enumerate(steps_of):
            j = section_at(dx, dy, -1)
            landed = wall.at[j // 2, lax.rem(j, 2), half, mine_z]
            remote(landed, landed, wd_send.at[n], wd_recv.at[j], on_section(j)).wait_recv()
        for way in range(2):
            part = wall.at[:, :, half, onward_z(way, odd)]
            go(remote(part, part, wz_send.at[way], wz_recv.at[way], z_next(way)))
        part = wall.at[:, :, half, mine_z]
        go(remote(part, part, wc_send.at[1], wc_recv.at[1], on_dp(mate)))

    def gather_y():
        for way in range(2):
            row = wall.at[:, 1 - yl, half, onward(way)]
            remote(row, row, wy_send.at[way], wy_recv.at[way], y_next(way)).wait_recv()
        row = wall.at[:, 1 - yl, half, near]
        go(remote(row, row, wc_send.at[2], wc_recv.at[2], on_dp(mate)))

    def gather_z():
        for way in range(2):
            part = wall.at[:, :, half, onward_z(way, 1 - odd)]
            remote(part, part, wz_send.at[way], wz_recv.at[way], z_next(way)).wait_recv()
        part = wall.at[:, :, half, theirs_z]
        go(remote(part, part, wc_send.at[3], wc_recv.at[3], on_dp(mate)))

    def project_near():
        for n, line in ((0, yl), (2, 1 - yl)):
            row = wall.at[:, line, other_half, near]
            remote(row, row, wc_send.at[n], wc_recv.at[n], on_dp(mate)).wait_recv()
        return over_last(lhs[:, : D // 2], wall[:, :, :, : D // 2].reshape(NL, D // 2))

    def project_rest(n, cols):
        part = wall.at[:, :, other_half, cols]
        remote(part, part, wc_send.at[n], wc_recv.at[n], on_dp(mate)).wait_recv()
        return over_last(lhs[:, cols], wall[:, :, :, cols].reshape(NL, E))

    def piece_norm():
        for n in range(2):
            loads[n].wait()

        def squares(i, acc):
            xf = lhs[0 : 2 * T, pl.ds(pl.multiple_of(i * 128, 128), 128)].astype(F32)
            return acc + xf * xf

        total = lax.fori_loop(0, D // 128, squares, jnp.zeros((2 * T, 128), F32), unroll=2)
        scale = lax.rsqrt(jnp.sum(total, axis=-1, keepdims=True) * (1.0 / D) + EPS)
        wide = jnp.broadcast_to(scale, (2 * T, 128))
        scale_v[...] = wide
        scale_t[...] = wide.T[0:8]

    def piece_hidden():
        for n in range(2, 5):
            loads[n].wait()

        def normed(i, carry):
            cols = pl.ds(pl.multiple_of(i * 128, 128), 128)
            for r in range(2):
                rows = slice(r * T, (r + 1) * T)
                nf = lhs[rows, cols].astype(F32) * scale_v[rows, :]
                hv[rows, cols] = (nf * gv[r : r + 1, cols]).astype(BF16)
                lhs[2 * T + r * R : 2 * T + (r + 1) * R, cols] = (
                    iv[r, :, cols].astype(F32) * gv[r : r + 1, cols]
                ).astype(BF16)
            return carry

        lax.fori_loop(0, D // 128, normed, 0)

    def piece_down():
        for r in range(2):
            rows = slice(r * T, (r + 1) * T)
            pre = over_last(hv[rows, :], iv[r])
            pre_v[:, r * R : (r + 1) * R] = pre
            early[:, r * R : (r + 1) * R] = pre
        pre = pre_v[...].T
        pre_t[...] = pre
        active = pre * jax.nn.sigmoid(pre)
        for r in range(2):
            act_t[r] = active[r * R : (r + 1) * R].astype(BF16)
        same[:, 0:T] = act_t[0]
        for i in range(1, S):
            j = peer(i)
            replica = jnp.where(j > me, 0, 1)
            rows = pl.ds(pl.multiple_of(jnp.where(j > me, me, mirror) * R, R), R)
            lanes = pl.ds(pl.multiple_of(replica * T, T), T)
            go(remote(act_t.at[replica], low.at[rows, lanes], t_send.at[i], t_recv.at[me], on_section(j)))
        go(remote(act_t.at[1], same.at[:, pl.ds(T, T)], g_send.at[0], g_recv.at[0], on_section(mirror)))

    def piece_up():
        for n in range(5, 7):
            loads[n].wait()
        for r in range(2):
            rows = slice(r * T, (r + 1) * T)
            early[:, (2 + r) * R : (3 + r) * R] = over_last(tv[rows, :], ov[r])
        for i in range(1, S):
            j = peer(i)
            rows = pl.ds(pl.multiple_of(j * Q, Q), Q)
            go(remote(early.at[rows], egot.at[me], e_send.at[i], e_recv.at[me], on_section(j)))
        egot[me] = early[pl.ds(pl.multiple_of(me * Q, Q), Q), :]

    piece_norm()
    piece_hidden()
    gather_row()
    gather_direct()
    piece_down()
    piece_up()
    across = project_rest(1, mine_z)
    gather_y()
    gather_z()
    across = across + project_near()
    across = across + project_rest(3, theirs_z)

    block = lax.broadcasted_iota(jnp.int32, (R, NL), 1) // R
    coup[...] = jnp.where(
        block < me, across[2 * T : 2 * T + R], across[2 * T + R :]
    ).astype(BF16)
    lane = lax.broadcasted_iota(jnp.int32, (T, NL), 1)
    block = lane // R
    within = lax.rem(lane, R) // (R // 4)
    sc0 = scale_v[:T, 0:1]
    sc1 = scale_v[T:, 0:1]
    sc = jnp.where(within < 2, sc0, sc1)
    rounded = sc.astype(BF16).astype(F32)
    own = jnp.where(lax.rem(within, 2) == 0, rounded, sc - rounded)
    late[...] = jnp.where(
        block < me, across[:T] * (sc0 * sc0), jnp.where(block > me, across[T : 2 * T] * (sc1 * sc1), own)
    ).astype(BF16)
    for i in range(1, S):
        j = peer(i)
        rows = pl.ds(pl.multiple_of(j * Q, Q), Q)
        go(remote(coup, cgot.at[me], k_send.at[i], k_recv.at[me], on_section(j)))
        go(remote(late.at[rows], lgot.at[me], v_send.at[i], v_recv.at[me], on_section(j)))
    cgot[me] = coup[...]
    lgot[me] = late[pl.ds(pl.multiple_of(me * Q, Q), Q), :]

    remote(act_t.at[1], same.at[:, pl.ds(T, T)], g_send.at[0], g_recv.at[0], on_section(mirror)).wait_recv()
    for q in range(NY):
        term = dot(same[...], tv[:, chunk(q)])
        for h in range(2):
            own_s[h, :, chunk(q)] = term[h * H : (h + 1) * H]
    go(remote(own_s.at[1 - core], own_r, o_send.at[0], o_recv.at[0], on_dp(mate)))

    for i in range(1, S):
        j = peer(S - i)
        remote(early.at[pl.ds(0, Q)], egot.at[j], e_send.at[i], e_recv.at[j], on_section(j)).wait_recv()
    pre = egot[:, :, 0 : 2 * R]
    sig = jax.nn.sigmoid(pre)
    slope = sig * (1.0 + pre * (1.0 - sig))
    for i in range(1, S):
        j = peer(S - i)
        remote(coup, cgot.at[j], k_send.at[i], k_recv.at[j], on_section(j)).wait_recv()
        remote(late.at[pl.ds(0, Q)], lgot.at[j], v_send.at[i], v_recv.at[j], on_section(j)).wait_recv()

    acc = [jnp.zeros((Q, NL), F32), jnp.zeros((Q, NL), F32)]
    for turn in range(S):
        for r in range(2):
            k = S - 1 - turn if r == 0 else turn
            lanes = slice(r * R, (r + 1) * R)
            up = egot[k, :, (2 + r) * R : (3 + r) * R]
            if turn > 0:
                up = up + acc[r][:, k * R : (k + 1) * R]
            delta = (up * slope[k, :, lanes]).astype(BF16)
            ans[k, :, lanes] = delta
            if turn < S - 1:
                inner = jnp.sum(delta.astype(F32) * pre[k, :, lanes], axis=-1, keepdims=True) * (1.0 / D)
                first = k * R + r * H
                sc = lgot[k, :, first : first + 1].astype(F32)
                sc = sc + lgot[k, :, first + R // 4 : first + R // 4 + 1].astype(F32)
                acc[r] = acc[r] + sc * dot(delta, cgot[k]) - inner * lgot[k].astype(F32)
    for i in range(1, S):
        j = peer(i)
        go(remote(ans.at[j], back.at[me], a_send.at[i], a_recv.at[me], on_section(j)))
    back[me] = ans[me]
    for i in range(1, S):
        j = peer(S - i)
        rows = pl.ds(pl.multiple_of(jnp.where(j < me, j, S - 1 - j) * R, R), R)
        lanes = pl.ds(pl.multiple_of(jnp.where(j < me, 0, T), T), T)
        remote(act_t.at[0], low.at[rows, lanes], t_send.at[i], t_recv.at[j], on_section(j)).wait_recv()
    lower = low[...].astype(F32)
    for i in range(1, S):
        j = peer(S - i)
        remote(ans.at[j], back.at[j], a_send.at[i], a_recv.at[j], on_section(j)).wait_recv()

    answer = back[...].reshape(T, 128)
    deltas = [answer[:, r * R : (r + 1) * R] for r in range(2)]
    turned = answer[:, 0 : 2 * R].astype(F32).T.astype(BF16)
    for r in range(2):
        tokens = slice(r * T, (r + 1) * T)
        seen = lower[:, tokens]
        tall = turned[r * R : (r + 1) * R].astype(F32) * pre_t[r * R : (r + 1) * R]
        sc = scale_t[0:1, tokens]
        pull = jnp.sum(tall, axis=0, keepdims=True) * (-1.0 / D) * (sc * sc)
        mix[:, tokens] = (seen * pull).astype(BF16)
        scaled = (deltas[r].astype(F32) * scale_v[tokens, 0:1]).astype(BF16)
        mix[:, 2 * T + r * R : 2 * T + (r + 1) * R] = dot(low[:, tokens], scaled).astype(BF16)
    W = min(512, CH)

    def terms(q):
        def part(i, carry):
            cols = pl.ds(pl.multiple_of(q * CH + i * W, W), W)
            below = dot(mix[...], lhs[:, cols]).astype(BF16)
            for j in range(S):
                for h in range(2):
                    es[h, j // 2, j % 2, :, cols] = below[j * R + h * H : j * R + (h + 1) * H]
            return carry

        lax.fori_loop(0, CH // W, part, 0)
        go(remote(
            es.at[1 - core, :, :, :, chunk(q)], pe.at[:, :, :, chunk(q)],
            c_send.at[q], c_recv.at[q], on_dp(mate),
        ))

    def down_terms(q):
        def part(i, carry):
            cols = pl.ds(pl.multiple_of(i * W, W), W)
            for r in range(2):
                rows = slice(r * T, (r + 1) * T)
                term = dot(turned[r * R : (r + 1) * R], hv[rows, cols]).astype(BF16)
                for h in range(2):
                    ds[h, r, :, cols] = term[h * H : (h + 1) * H]
            return carry

        lax.fori_loop(0, D // W, part, 0)
        go(remote(ds.at[1 - core], dr, d_send.at[0], d_recv.at[0], on_dp(mate)))

    def down_send(q):
        remote(dr, dr, d_send.at[0], d_recv.at[0], on_dp(mate)).wait_recv()
        dr[...] = (ds[core].astype(F32) + dr[...].astype(F32)).astype(BF16)
        go(remote(dr.at[1], fr, f_send.at[0], f_recv.at[0], on_section(mirror)))

    def step_y(q):
        landed = pe.at[:, :, :, chunk(q)]
        remote(landed, landed, c_send.at[q], c_recv.at[q], on_dp(mate)).wait_recv()
        ss[:, :, :, chunk(q)] = (
            es[core, :, :, :, chunk(q)].astype(F32) + pe[:, :, :, chunk(q)].astype(F32)
        ).astype(BF16)
        for way in range(2):
            go(remote(
                ss.at[:, 1 - yl, :, side(q, way)], yb.at[:, :, side(q, way)],
                ty_send.at[way, q], ty_recv.at[way, q], y_next(way),
            ))

    def step_x(q):
        for way in range(2):
            landed = yb.at[:, :, side(q, way)]
            remote(landed, landed, ty_send.at[way, q], ty_recv.at[way, q], y_next(way)).wait_recv()
        xs[:, :, chunk(q)] = (
            ss[:, yl, :, chunk(q)].astype(F32) + yb[:, :, chunk(q)].astype(F32)
        ).astype(BF16)
        for i in range(1, X):
            k = x_peer(i)
            go(remote(xs.at[k, :, chunk(q)], xr.at[x, :, chunk(q)], tx_send.at[i, q], tx_recv.at[x, q], in_row(k)))

    def step_z(q):
        for i in range(1, X):
            k = x_peer(X - i)
            landed = xr.at[k, :, chunk(q)]
            remote(landed, landed, tx_send.at[i, q], tx_recv.at[k, q], in_row(k)).wait_recv()
        if q == 0:
            remote(fr, fr, f_send.at[0], f_recv.at[0], on_section(mirror)).wait_recv()
            remote(own_r, own_r, o_send.at[0], o_recv.at[0], on_dp(mate)).wait_recv()
        whole = own_s[core, :, chunk(q)] + own_r[:, chunk(q)] + xs[x, :, chunk(q)].astype(F32)
        for k in range(X):
            whole = whole + xr[k, :, chunk(q)].astype(F32)
        zs[0:H, chunk(q)] = whole.astype(BF16)
        zs[H:R, chunk(q)] = (dr[0, :, chunk(q)].astype(F32) + fr[:, chunk(q)].astype(F32)).astype(BF16)
        for i in range(1, NZ):
            k = lax.rem(z + i, NZ)
            source = pl.ds(pl.multiple_of(q * CH + k * 128, 128), 128)
            go(remote(
                zs.at[:, source], zr.at[z, :, pl.ds(q * 128, 128)],
                z_send.at[i, q], z_recv.at[z, q], on_dp(place(yh, k)),
            ))
        zr[z, :, q * 128 : (q + 1) * 128] = zs[:, pl.ds(pl.multiple_of(q * CH + z * 128, 128), 128)]

    def y_copy(q, c):
        return remote(
            zt.at[q], yr.at[core, yh], y_send.at[c, q], y_recv.at[core, yh], on_dp(place(q, z, c))
        )

    def on_other(q, c, act):
        @pl.when((yh != q) | (core != c))
        def _():
            act()

    def step_yh(q):
        for i in range(1, NZ):
            k = lax.rem(z + NZ - i, NZ)
            landed = zr.at[k, :, pl.ds(q * 128, 128)]
            remote(landed, landed, z_send.at[i, q], z_recv.at[k, q], on_dp(place(yh, k))).wait_recv()
        whole = zr[0, :, q * 128 : (q + 1) * 128].astype(F32)
        for k in range(1, NZ):
            whole = whole + zr[k, :, q * 128 : (q + 1) * 128].astype(F32)
        zt[q] = whole

        for c in range(CORES):
            on_other(q, c, lambda: y_copy(q, c).start())

        @pl.when(yh == q)
        def _():
            yr[core, q] = zt[q]

    steps = [(terms, 0.0), (step_y, 1.1), (step_x, 3.9), (step_z, 6.4), (step_yh, 9.4)]
    order = [(q + late_by, step, q) for step, late_by in steps for q in range(NY)]
    order += [(0.5, down_terms, 0), (1.15, down_send, 0)]
    for _, step, q in sorted(order, key=lambda entry: entry[0]):
        step(q)

    for c in range(CORES):
        for k in range(NY):
            landed = yr.at[c, k]
            copy = remote(landed, landed, y_send.at[c, k], y_recv.at[c, k], on_dp(place(k, z, c)))
            on_other(k, c, copy.wait_recv)
    for c in range(CORES):
        whole = yr[c, 0]
        for k in range(1, NY):
            whole = whole + yr[c, k]
        out[c] = whole

    for copy in sent:
        copy.wait_send()
    for q in range(NY):
        for c in range(CORES):
            on_other(q, c, y_copy(q, c).wait_send)


def own_columns(parts, out_in, out_out):
    core = lax.rem(lax.axis_index("dp"), CORES)
    H = parts.shape[1] // 2
    for h in range(2):
        chosen = jnp.where(core == 0, parts[h, :, :64], parts[h, :, 64:])
        out_out[h * H : (h + 1) * H, :] = chosen[:H]
        out_in[h * H : (h + 1) * H, :] = chosen[H:]


def on_device(rings, saved, top_grad, gains, adapter_in, adapter_out):
    S = lax.axis_size("section")
    NY, NZ = rings
    _, _, T, D = saved.shape
    R = adapter_in.shape[3]
    X, NL, H, Q = S // 2, S * R, R // 2, T // S
    dma = pltpu.SemaphoreType.DMA
    scratch = [
        pltpu.VMEM((2 * T + 2 * R, D), BF16),
        pltpu.VMEM((2 * T, D), BF16),
        pltpu.VMEM((2 * T, D), BF16),
        pltpu.VMEM((2, D), F32),
        pltpu.VMEM((2, R, D), BF16),
        pltpu.VMEM((2, R, D), BF16),
        pltpu.VMEM((X, 2, R, D), BF16),
        pltpu.VMEM((2 * T, 128), F32),
        pltpu.VMEM((8, 2 * T), F32),
        pltpu.VMEM((T, 2 * R), F32),
        pltpu.VMEM((2 * R, T), F32),
        pltpu.VMEM((NL, 2 * T + 2 * R), BF16),
        pltpu.VMEM((T, 4 * R), F32),
        pltpu.VMEM((T, NL), BF16),
        pltpu.VMEM((R, NL), BF16),
        pltpu.VMEM((S, Q, 4 * R), F32),
        pltpu.VMEM((S, Q, NL), BF16),
        pltpu.VMEM((S, R, NL), BF16),
        pltpu.VMEM((2, R, T), BF16),
        pltpu.VMEM((NL, 2 * T), BF16),
        pltpu.VMEM((R, 2 * T), BF16),
        pltpu.VMEM((S, Q, 128), BF16),
        pltpu.VMEM((S, Q, 128), BF16),
        pltpu.VMEM((2, H, D), F32),
        pltpu.VMEM((H, D), F32),
        pltpu.VMEM((2, 2, H, D), BF16),
        pltpu.VMEM((2, H, D), BF16),
        pltpu.VMEM((2, X, 2, H, D), BF16),
        pltpu.VMEM((X, 2, H, D), BF16),
        pltpu.VMEM((X, 2, H, D), BF16),
        pltpu.VMEM((X, H, D), BF16),
        pltpu.VMEM((X, H, D), BF16),
        pltpu.VMEM((X, H, D), BF16),
        pltpu.VMEM((H, D), BF16),
        pltpu.VMEM((R, D), BF16),
        pltpu.VMEM((NZ, R, NY * 128), BF16),
        pltpu.VMEM((NY, R, 128), F32),
        pltpu.VMEM((CORES, NY, R, 128), F32),
        dma((9,)),
    ]
    scratch += [dma((X,))] * 2 + [dma((S,))] * 2 + [dma((2,))] * 4 + [dma((4,))] * 2
    scratch += [dma((S,))] * 4 + [dma((1,))] * 2 + [dma((S,))] * 4
    scratch += [dma((S,))] * 2 + [dma((1,))] * 4 + [dma((NY,))] * 2 + [dma((2, NY))] * 2
    scratch += [dma((X, NY))] * 2 + [dma((1,))] * 2
    scratch += [dma((NZ, NY))] * 2 + [dma((CORES, NY))] * 2
    half = D // (NY * NZ * CORES)
    vmem = pl.BlockSpec(memory_space=pltpu.VMEM)
    parts = pl.pallas_call(
        partial(kernel, (S, NY, NZ, T, D, R)),
        out_shape=jax.ShapeDtypeStruct((2, R, 128), F32),
        in_specs=[pl.BlockSpec(memory_space=pl.ANY)] * 5,
        out_specs=vmem,
        scratch_shapes=scratch,
        compiler_params=pltpu.CompilerParams(
            collective_id=0, has_side_effects=True, vmem_limit_bytes=56 * 2**20
        ),
        cost_estimate=pl.CostEstimate(
            flops=4 * 10**9, bytes_accessed=6 * 2**20, transcendentals=2 * T * R
        ),
    )(saved, top_grad, gains, jnp.swapaxes(adapter_in, 2, 3), adapter_out)
    shape = jax.ShapeDtypeStruct((R, half), F32)
    grad_in, grad_out = pl.pallas_call(
        own_columns, out_shape=(shape, shape), in_specs=[vmem], out_specs=(vmem, vmem)
    )(parts)
    return (grad_in.T[None], grad_out[None])


def solution(mesh):
    in_specs = (
        P("section", None, "dp", None),
        P(None, "dp", None),
        P("section", None, None),
        P("section", None, None, None),
        P("section", None, None, None),
    )
    out_specs = (P("section", "dp", None), P("section", None, "dp"))
    return jax.shard_map(
        partial(on_device, RINGS[mesh.shape["dp"]]),
        mesh=mesh, in_specs=in_specs, out_specs=out_specs, check_vma=False,
    )
```
